1024 devices in a mesh: row: 32 (over y_lo, z), col: 4 (over y_hi), depth: 8 (over x, core).
Axes of the slice: x: 4, y: 8 (y_hi: 4, y_lo: 2; y = y_hi * 2 + y_lo), z: 16, core: 2. Of those that a mesh axis runs over, the one named last changes fastest.
Arguments:
- tokens: bfloat16 [256, 8192], P('row', ('col', 'depth')), may hold values from -6 to 6
- grad_out: bfloat16 [256, 8192], P('row', ('col', 'depth')), may hold values from -6 to 6
- gate_weight: bfloat16 [8192, 28672], P(('col', 'depth'), 'row'), may hold values from -0.0625 to 0.0625
- up_weight: bfloat16 [8192, 28672], P(('col', 'depth'), 'row'), may hold values from -0.0625 to 0.0625
- down_weight: bfloat16 [28672, 8192], P('row', ('col', 'depth')), may hold values from -0.03125 to 0.03125
Outputs:
- layer_out: bfloat16 [256, 8192], P('row', ('col', 'depth'))
- grad_tokens: bfloat16 [256, 8192], P('row', ('col', 'depth'))
- grad_gate: bfloat16 [8192, 28672], P(('col', 'depth'), 'row')
- grad_up: bfloat16 [8192, 28672], P(('col', 'depth'), 'row')
- grad_down: bfloat16 [28672, 8192], P('row', ('col', 'depth'))
The draws below stay inside these ranges and needn't reach their ends.
All inputs are finite; a program needn't handle non-finite values.
Results may differ from the reference program's by a relative error of at most 0.0049.
Values may be sent and summed in bfloat16 or wider, within the bound.
A program may use at most 32 MiB of HBM per device.

```python
import jax
import jax.numpy as jnp

D = 8192
FF = 28672
TOKENS = 256


def block_levels(key, extent, cuts, smallest, largest):
    loudness, own = 1.0, jax.random.fold_in(key, 6)
    for axis_at, parts in cuts:
        draws = jnp.exp(jax.random.uniform(jax.random.fold_in(own, axis_at), (parts,), jnp.float32, smallest / len(cuts), largest / len(cuts)))
        loudness = loudness * jnp.repeat(draws, extent[axis_at] // parts).reshape([-1 if axis == axis_at else 1 for axis in range(len(extent))])
    return loudness


def centred(own_key, dims, spread, bound, shards=(), kind=jnp.bfloat16):
    gain = block_levels(own_key, dims, shards, -0.22, 0.18) if shards else 1.0
    result = jax.random.normal(own_key, dims, jnp.float32) * spread * gain
    return jnp.minimum(jnp.maximum(result, -bound), bound).astype(kind)


def setup_inputs(seed: int = 0) -> dict:
    key_list = jax.random.split(jax.random.key(seed), 6)
    return {
        "tokens": centred(key_list[0], (TOKENS, D), 1.0, 6.0, ((0, 32), (1, 32))),
        "grad_out": centred(key_list[1], (TOKENS, D), 1.0, 6.0, ((0, 32), (1, 32))),
        "gate_weight": centred(key_list[2], (D, FF), D ** -0.5, 0.0625, ((0, 32), (1, 32))),
        "up_weight": centred(key_list[3], (D, FF), D ** -0.5, 0.0625, ((0, 32), (1, 32))),
        "down_weight": centred(key_list[4], (FF, D), FF ** -0.5, 0.03125, ((0, 32), (1, 32))),
    }


def reference(tokens, grad_out, gate_weight, up_weight, down_weight):
    gate_pre = jnp.dot(tokens, gate_weight, preferred_element_type=jnp.float32)
    up_proj = jnp.dot(tokens, up_weight, preferred_element_type=jnp.float32)
    sigmoid_gate = jax.nn.sigmoid(gate_pre)
    activated = gate_pre * sigmoid_gate
    hidden = (activated * up_proj).astype(jnp.bfloat16)
    layer_out = jnp.dot(hidden, down_weight, preferred_element_type=jnp.float32).astype(jnp.bfloat16)
    d_hidden = jnp.dot(grad_out, down_weight.T, preferred_element_type=jnp.float32)
    d_gate = (d_hidden * up_proj * sigmoid_gate * (1.0 + gate_pre * (1.0 - sigmoid_gate))).astype(jnp.bfloat16)
    d_up = (d_hidden * activated).astype(jnp.bfloat16)
    grad_down = jnp.dot(hidden.T, grad_out, preferred_element_type=jnp.float32).astype(jnp.bfloat16)
    grad_gate = jnp.dot(tokens.T, d_gate, preferred_element_type=jnp.float32).astype(jnp.bfloat16)
    grad_up = jnp.dot(tokens.T, d_up, preferred_element_type=jnp.float32).astype(jnp.bfloat16)
    grad_tokens = (jnp.dot(d_gate, gate_weight.T, preferred_element_type=jnp.float32)
                   + jnp.dot(d_up, up_weight.T, preferred_element_type=jnp.float32)).astype(jnp.bfloat16)
    return layer_out, grad_tokens, grad_gate, grad_up, grad_down
```

```python
import jax
import jax.numpy as jnp
from jax import lax
from jax.experimental import pallas as pl
from jax.experimental.pallas import tpu as pltpu
from jax.sharding import PartitionSpec as P

MESH = pl.DeviceIdType.MESH
F32 = jnp.float32
BF16 = jnp.bfloat16
FAR_FIRST = (2, 1, 3, 0)


def dot(left, right, left_dim, right_dim):
    return lax.dot_general(
        left, right, (((left_dim,), (right_dim,)), ((), ())), preferred_element_type=F32
    )


def kernel(
    tok_ref, grad_ref, gw_hbm, uw_hbm, dw_hbm,
    lo_ref, gt_ref, gg_hbm, gu_hbm, gd_hbm,
    gw, uw, dw, gath, part, core_in, pack, plane_in, own, acts, p4, y_in, zpack, z_in, gg, gu, gd,
    load_sem, store_sem,
    tz_send, tz_recv, ty_send, ty_recv,
    pc_send, pc_recv, pp_send, pp_recv,
    ap_send, ap_recv, ac_send, ac_recv,
    oy_send, oy_recv, oz_send, oz_recv,
):
    row, col, depth = lax.axis_index("row"), lax.axis_index("col"), lax.axis_index("depth")
    y_lo, z = lax.div(row, 16), lax.rem(row, 16)
    x, core = lax.div(depth, 2), lax.rem(depth, 2)
    ff = gw.shape[1]
    d = gw.shape[0]

    def z_dev(other):
        return (y_lo * 16 + other, col, depth)

    y_dev = ((1 - y_lo) * 16 + z, col, depth)
    core_dev = (row, col, x * 2 + 1 - core)

    def plane_dev(other_col, other_x):
        return (row, other_col, other_x * 2 + core)

    def remote(src, dst, send, recv, device):
        return pltpu.make_async_remote_copy(
            src_ref=src, dst_ref=dst, send_sem=send, recv_sem=recv,
            device_id=device, device_id_type=MESH,
        )

    def z_off(i):
        return 8 + lax.div(i + 1, 2) * (2 * lax.rem(i, 2) - 1)

    loads = [
        pltpu.make_async_copy(gw_hbm, gw, load_sem.at[0]),
        pltpu.make_async_copy(uw_hbm, uw, load_sem.at[1]),
        pltpu.make_async_copy(dw_hbm, dw, load_sem.at[2]),
    ]
    for load in loads:
        load.start()

    barrier = pltpu.get_barrier_semaphore()

    def greet_z(i, c):
        pl.semaphore_signal(barrier, inc=1, device_id=z_dev(lax.rem(z + z_off(i), 16)), device_id_type=MESH)
        return c

    def greet_plane(i, c):
        pl.semaphore_signal(
            barrier, inc=1,
            device_id=plane_dev(lax.rem(col + lax.div(i, 4), 4), lax.rem(x + lax.rem(i, 4), 4)),
            device_id_type=MESH,
        )
        return c

    lax.fori_loop(0, 15, greet_z, 0)
    lax.fori_loop(1, 16, greet_plane, 0)
    pl.semaphore_signal(barrier, inc=1, device_id=y_dev, device_id_type=MESH)
    pl.semaphore_signal(barrier, inc=1, device_id=core_dev, device_id_type=MESH)
    gath[row] = jnp.concatenate(
        [tok_ref[...].astype(F32), grad_ref[...].astype(F32)], axis=0
    ).astype(BF16)
    pl.semaphore_wait(barrier, 32)

    def tz_copy(i):
        return remote(
            gath.at[row], gath.at[row], tz_send.at[i], tz_recv.at[z],
            z_dev(lax.rem(z + z_off(i), 16)),
        )

    def ty_copy(src_z):
        slot = y_lo * 16 + src_z
        return remote(gath.at[slot], gath.at[slot], ty_send.at[src_z], ty_recv.at[src_z], y_dev)

    def tz_start(i, c):
        tz_copy(i).start()
        return c

    lax.fori_loop(0, 15, tz_start, 0)
    ty_copy(z).start()

    def tz_pass(k, c):
        src_z = lax.rem(z + 16 - z_off(14 - k), 16)
        slot = y_lo * 16 + src_z
        remote(gath.at[slot], gath.at[slot], tz_send.at[0], tz_recv.at[src_z], y_dev).wait_recv()
        ty_copy(src_z).start()
        return c

    lax.fori_loop(0, 15, tz_pass, 0)

    def ty_arrive(src_z, c):
        slot = (1 - y_lo) * 16 + src_z
        remote(gath.at[slot], gath.at[slot], ty_send.at[src_z], ty_recv.at[src_z], y_dev).wait_recv()
        return c

    lax.fori_loop(0, 16, ty_arrive, 0)
    for load in loads:
        load.wait()

    both = gath[...].astype(F32)
    tok_all = both[:, :8, :].reshape(256, d).astype(BF16)
    grad_all = both[:, 8:, :].reshape(256, d).astype(BF16)

    part[:, :, :, 0:ff] = dot(tok_all, gw[...], 1, 0).reshape(16, 2, 8, ff)
    part[:, :, :, ff:2 * ff] = dot(tok_all, uw[...], 1, 0).reshape(16, 2, 8, ff)
    part[:, :, :, 2 * ff:] = dot(grad_all, dw[...], 1, 1).reshape(16, 2, 8, ff)

    def pc_copy(q):
        chips = pl.ds(lax.rem(col + q, 4) * 4, 4)
        return remote(part.at[chips, 1 - core], core_in.at[chips], pc_send.at[q], pc_recv.at[q], core_dev)

    for q in FAR_FIRST:
        pc_copy(q).start()

    me = col * 4 + x

    def pp_copy(q, step):
        other_col, other_x = lax.rem(col + q, 4), lax.rem(x + step, 4)
        return remote(
            pack.at[other_col * 4 + other_x], plane_in.at[me],
            pp_send.at[q * 4 + step], pp_recv.at[me], plane_dev(other_col, other_x),
        )

    for q in FAR_FIRST:
        pc_copy(q).wait_recv()
        chips = pl.ds(lax.rem(col + q, 4) * 4, 4)
        pack[chips] = (part[chips, core] + core_in[chips]).astype(BF16)
        for step in FAR_FIRST:
            if q or step:
                pp_copy(q, step).start()

    def pp_arrive(i, total):
        src = lax.rem(col + lax.div(i, 4), 4) * 4 + lax.rem(x + lax.rem(i, 4), 4)
        remote(plane_in.at[src], plane_in.at[src], pp_send.at[0], pp_recv.at[src], core_dev).wait_recv()
        return total + plane_in[src].astype(F32)

    total = lax.fori_loop(1, 16, pp_arrive, part[me, core] + core_in[me])

    gate_pre = total[:, 0:ff]
    up_proj = total[:, ff:2 * ff]
    d_hidden = total[:, 2 * ff:]
    sig = jax.nn.sigmoid(gate_pre)
    share = me * 2 + core
    acts[share, :, 0:ff] = (gate_pre * sig * up_proj).astype(BF16)
    acts[share, :, ff:2 * ff] = (
        d_hidden * up_proj * sig * (1.0 + gate_pre * (1.0 - sig))
    ).astype(BF16)
    acts[share, :, 2 * ff:] = (d_hidden * gate_pre * sig).astype(BF16)

    def ap_copy(i):
        other_col, other_x = lax.rem(col + lax.div(i, 4), 4), lax.rem(x + lax.rem(i, 4), 4)
        return remote(
            acts.at[share], acts.at[share], ap_send.at[i], ap_recv.at[me], plane_dev(other_col, other_x)
        )

    def ac_copy(chip):
        slot = chip * 2 + core
        return remote(acts.at[slot], acts.at[slot], ac_send.at[chip], ac_recv.at[chip], core_dev)

    for q in FAR_FIRST:
        for step in FAR_FIRST:
            if q or step:
                ap_copy(q * 4 + step).start()
    ac_copy(me).start()

    def ap_pass(q):
        def body(i, c):
            src = lax.rem(col + q, 4) * 4 + lax.rem(x + i, 4)
            slot = src * 2 + core
            remote(acts.at[slot], acts.at[slot], ap_send.at[0], ap_recv.at[src], core_dev).wait_recv()
            ac_copy(src).start()
            return c
        return body

    for q in (0, 1, 3, 2):
        lax.fori_loop(0 if q else 1, 4, ap_pass(q), 0)

    def ac_arrive(chip, c):
        slot = chip * 2 + 1 - core
        remote(acts.at[slot], acts.at[slot], ac_send.at[chip], ac_recv.at[chip], core_dev).wait_recv()
        return c

    lax.fori_loop(0, 16, ac_arrive, 0)

    hid = acts[:, :, 0:ff].astype(F32).reshape(256, ff).astype(BF16)
    d_gate = acts[:, :, ff:2 * ff].astype(F32).reshape(256, ff).astype(BF16)
    d_up = acts[:, :, 2 * ff:].astype(F32).reshape(256, ff).astype(BF16)

    p4[:, :, :, 0:d] = dot(hid, dw[...], 1, 0).reshape(2, 16, 8, d)
    p4[:, :, :, d:] = (dot(d_gate, gw[...], 1, 1) + dot(d_up, uw[...], 1, 1)).reshape(2, 16, 8, d)

    z_hi, z_sub = lax.div(z, 4), lax.rem(z, 4)

    def oy_copy(q):
        zs = pl.ds(lax.rem(z_hi + q, 4) * 4, 4)
        return remote(p4.at[1 - y_lo, zs], y_in.at[zs], oy_send.at[q], oy_recv.at[q], y_dev)

    for q in FAR_FIRST:
        oy_copy(q).start()

    gg[...] = dot(tok_all, d_gate, 0, 0).astype(BF16)
    stores = [pltpu.make_async_copy(gg, gg_hbm, store_sem.at[0])]
    stores[0].start()

    def oz_copy(q, step):
        other = lax.rem(z_hi + q, 4) * 4 + lax.rem(z_sub + step, 4)
        return remote(
            zpack.at[other], z_in.at[z], oz_send.at[q * 4 + step], oz_recv.at[z], z_dev(other)
        )

    for q in FAR_FIRST:
        oy_copy(q).wait_recv()
        zs = pl.ds(lax.rem(z_hi + q, 4) * 4, 4)
        zpack[zs] = (p4[y_lo, zs] + y_in[zs]).astype(BF16)
        for step in FAR_FIRST:
            if q or step:
                oz_copy(q, step).start()

    gu[...] = dot(tok_all, d_up, 0, 0).astype(BF16)
    stores.append(pltpu.make_async_copy(gu, gu_hbm, store_sem.at[1]))
    stores[1].start()
    gd[...] = dot(hid, grad_all, 0, 0).astype(BF16)
    stores.append(pltpu.make_async_copy(gd, gd_hbm, store_sem.at[2]))
    stores[2].start()

    def oz_arrive(i, total):
        src = lax.rem(z + i, 16)
        remote(z_in.at[src], z_in.at[src], oz_send.at[0], oz_recv.at[src], y_dev).wait_recv()
        return total + z_in[src].astype(F32)

    result = lax.fori_loop(1, 16, oz_arrive, p4[y_lo, z] + y_in[z])
    lo_ref[...] = result[:, 0:d].astype(BF16)
    gt_ref[...] = result[:, d:].astype(BF16)

    def tz_left(i, c):
        tz_copy(i).wait_send()
        return c

    def ty_left(i, c):
        ty_copy(i).wait_send()
        return c

    def ap_left(i, c):
        ap_copy(i).wait_send()
        return c

    def ac_left(i, c):
        ac_copy(i).wait_send()
        return c

    lax.fori_loop(0, 15, tz_left, 0)
    lax.fori_loop(0, 16, ty_left, 0)
    lax.fori_loop(1, 16, ap_left, 0)
    lax.fori_loop(0, 16, ac_left, 0)
    for q in FAR_FIRST:
        pc_copy(q).wait_send()
        oy_copy(q).wait_send()
        for step in FAR_FIRST:
            if q or step:
                pp_copy(q, step).wait_send()
                oz_copy(q, step).wait_send()
    for store in stores:
        store.wait()


def per_device(tokens, grad_out, gate_weight, up_weight, down_weight):
    d, ff = gate_weight.shape
    vmem = pl.BlockSpec(memory_space=pltpu.VMEM)
    hbm = pl.BlockSpec(memory_space=pl.ANY)
    dma = pltpu.SemaphoreType.DMA
    return pl.pallas_call(
        kernel,
        out_shape=(
            jax.ShapeDtypeStruct((8, d), BF16),
            jax.ShapeDtypeStruct((8, d), BF16),
            jax.ShapeDtypeStruct((d, ff), BF16),
            jax.ShapeDtypeStruct((d, ff), BF16),
            jax.ShapeDtypeStruct((ff, d), BF16),
        ),
        in_specs=[vmem, vmem, hbm, hbm, hbm],
        out_specs=(vmem, vmem, hbm, hbm, hbm),
        scratch_shapes=[
            pltpu.VMEM((d, ff), BF16),
            pltpu.VMEM((d, ff), BF16),
            pltpu.VMEM((ff, d), BF16),
            pltpu.VMEM((32, 16, d), BF16),
            pltpu.VMEM((16, 2, 8, 3 * ff), F32),
            pltpu.VMEM((16, 8, 3 * ff), F32),
            pltpu.VMEM((16, 8, 3 * ff), BF16),
            pltpu.VMEM((16, 8, 3 * ff), BF16),
            pltpu.VMEM((8, 3 * ff), F32),
            pltpu.VMEM((32, 8, 3 * ff), BF16),
            pltpu.VMEM((2, 16, 8, 2 * d), F32),
            pltpu.VMEM((16, 8, 2 * d), F32),
            pltpu.VMEM((16, 8, 2 * d), BF16),
            pltpu.VMEM((16, 8, 2 * d), BF16),
            pltpu.VMEM((d, ff), BF16),
            pltpu.VMEM((d, ff), BF16),
            pltpu.VMEM((ff, d), BF16),
            dma((3,)), dma((3,)),
            dma((15,)), dma((16,)), dma((16,)), dma((16,)),
            dma((4,)), dma((4,)), dma((16,)), dma((16,)),
            dma((16,)), dma((16,)), dma((16,)), dma((16,)),
            dma((4,)), dma((4,)), dma((16,)), dma((16,)),
        ],
        compiler_params=pltpu.CompilerParams(
            collective_id=0, has_side_effects=True, vmem_limit_bytes=44 << 20
        ),
        name="swiglu_exchange",
    )(tokens, grad_out, gate_weight, up_weight, down_weight)


def solution(mesh):
    acts = P("row", ("col", "depth"))
    weights = P(("col", "depth"), "row")
    return jax.shard_map(
        per_device,
        mesh=mesh,
        in_specs=(acts, acts, weights, weights, acts),
        out_specs=(acts, acts, weights, weights, acts),
        check_vma=False,
    )
```

```python
import functools
import jax
import jax.numpy as jnp
from jax import lax
from jax.experimental import pallas as pl
from jax.experimental.pallas import tpu as pltpu
from jax.sharding import PartitionSpec as P

MESH = pl.DeviceIdType.MESH
F32 = jnp.float32
BF16 = jnp.bfloat16
FAR = (2, 1, 3)
NEAR = (1, 3, 2)


def dot(left, right, left_dim, right_dim):
    return lax.dot_general(
        left, right, (((left_dim,), (right_dim,)), ((), ())), preferred_element_type=F32
    )


def kernel(
    tok_hbm, grad_hbm, gw_hbm, uw_hbm, dw_hbm,
    lo_ref, gt_ref, gg_hbm, gu_hbm, gd_hbm,
    gw, uw, dw, gath0, gath1,
    part0, part1, core_in0, core_in1, pack0, pack1, x_in0, x_in1, y_out0, y_out1, y_in0, y_in1,
    acts0, acts1, p4, n_in, zpack, z_in, gg, gu, gd,
    load_sem, store_sem,
    tz_send, tz_recv, ty_send, ty_recv,
    sc_send, sc_recv, sx_send, sx_recv, sy_send, sy_recv,
    ay_send, ay_recv, ax_send, ax_recv, ac_send, ac_recv,
    on_send, on_recv, oz_send, oz_recv,
):
    row, col, depth = lax.axis_index("row"), lax.axis_index("col"), lax.axis_index("depth")
    y_lo, z = lax.div(row, 16), lax.rem(row, 16)
    x, core = lax.div(depth, 2), lax.rem(depth, 2)
    d, ff = gw.shape
    gath = (gath0, gath1)
    part, core_in, pack = (part0, part1), (core_in0, core_in1), (pack0, pack1)
    x_in, y_out, y_in, acts = (x_in0, x_in1), (y_out0, y_out1), (y_in0, y_in1), (acts0, acts1)

    def z_dev(other):
        return (y_lo * 16 + other, col, depth)

    def col_dev(other):
        return (row, other, depth)

    def x_dev(other):
        return (row, col, other * 2 + core)

    next_dev = ((1 - y_lo) * 16 + z, col, depth)
    core_dev = (row, col, x * 2 + 1 - core)

    def remote(src, dst, send, recv, device):
        return pltpu.make_async_remote_copy(
            src_ref=src, dst_ref=dst, send_sem=send, recv_sem=recv,
            device_id=device, device_id_type=MESH,
        )

    def arrived(ref, recv):
        remote(ref, ref, load_sem.at[0], recv, core_dev).wait_recv()

    def left(ref, send):
        remote(ref, ref, send, load_sem.at[0], core_dev).wait_send()

    def z_off(i):
        return 8 + lax.div(i + 1, 2) * (2 * lax.rem(i, 2) - 1)

    def col_at(q):
        return lax.rem(col + q, 4)

    def x_at(step):
        return lax.rem(x + step, 4)

    own_loads = [
        pltpu.make_async_copy(tok_hbm, gath0.at[row], load_sem.at[0]),
        pltpu.make_async_copy(grad_hbm, gath1.at[row], load_sem.at[1]),
    ]
    loads = [
        pltpu.make_async_copy(gw_hbm, gw, load_sem.at[2]),
        pltpu.make_async_copy(uw_hbm, uw, load_sem.at[3]),
        pltpu.make_async_copy(dw_hbm, dw, load_sem.at[4]),
    ]
    for load in own_loads + loads:
        load.start()

    barrier = pltpu.get_barrier_semaphore()

    def greet(device):
        pl.semaphore_signal(barrier, inc=1, device_id=device, device_id_type=MESH)

    def greet_z(i, c):
        greet(z_dev(lax.rem(z + z_off(i), 16)))
        return c

    lax.fori_loop(0, 15, greet_z, 0)
    for step in FAR:
        greet(col_dev(col_at(step)))
        greet(x_dev(x_at(step)))
    greet(next_dev)
    greet(core_dev)
    for load in own_loads:
        load.wait()
    pl.semaphore_wait(barrier, 23)

    def pass_on(p, src_z):
        slot = gath[p].at[y_lo * 16 + src_z]
        remote(slot, slot, ty_send.at[p], ty_recv.at[p], next_dev).start()

    def gather_start(p):
        def body(i, c):
            slot = gath[p].at[row]
            remote(slot, slot, tz_send.at[p], tz_recv.at[p * 16 + z], z_dev(lax.rem(z + z_off(i), 16))).start()
            return c
        lax.fori_loop(0, 15, body, 0)
        pass_on(p, z)

    def gather_pass(p):
        def body(k, c):
            src_z = lax.rem(z + 16 - z_off(14 - k), 16)
            arrived(gath[p].at[y_lo * 16 + src_z], tz_recv.at[p * 16 + src_z])
            pass_on(p, src_z)
            return c
        lax.fori_loop(0, 15, body, 0)

    def gather_all(p):
        arrived(gath[p].at[pl.ds((1 - y_lo) * 16, 16)], ty_recv.at[p])
        return gath[p][...].astype(F32).reshape(256, d).astype(BF16)

    def sums_start(p):
        for q in FAR + (0,):
            chips = pl.ds(col_at(q) * 4, 4)
            remote(
                part[p].at[chips, 1 - core], core_in[p].at[chips],
                sc_send.at[p], sc_recv.at[p * 4 + q], core_dev,
            ).start()

    def sums_x(p, q):
        first = col_at(q) * 4
        chips = pl.ds(first, 4)
        arrived(core_in[p].at[chips], sc_recv.at[p * 4 + q])
        pack[p][chips] = (part[p][chips, core] + core_in[p][chips]).astype(BF16)
        for step in FAR:
            remote(
                pack[p].at[first + x_at(step)], x_in[p].at[first + x],
                sx_send.at[p], sx_recv.at[p * 4 + col_at(q)], x_dev(x_at(step)),
            ).start()

    def sums_y(p, q):
        first = col_at(q) * 4
        arrived(x_in[p].at[pl.ds(0, 3)], sx_recv.at[p * 4 + col_at(q)])
        total = part[p][first + x, core] + core_in[p][first + x]
        for step in FAR:
            total = total + x_in[p][first + x_at(step)].astype(F32)
        y_out[p][col_at(q)] = total
        if q:
            remote(
                y_out[p].at[col_at(q)], y_in[p].at[col], sy_send.at[p], sy_recv.at[p], col_dev(col_at(q))
            ).start()

    def sums_total(p):
        arrived(y_in[p].at[pl.ds(0, 3)], sy_recv.at[p])
        total = y_out[p][col]
        for q in FAR:
            total = total + y_in[p][col_at(q)]
        return total

    def acts_x(p, q):
        slot = acts[p].at[col_at(q) * 4 + x, core]
        for step in FAR:
            remote(
                slot, slot, ax_send.at[p], ax_recv.at[p * 4 + col_at(q)], x_dev(x_at(step))
            ).start()

    def acts_start(p):
        slot = acts[p].at[col * 4 + x, core]
        for q in FAR:
            remote(slot, slot, ay_send.at[p], ay_recv.at[p * 4 + col], col_dev(col_at(q))).start()
        acts_x(p, 0)

    def acts_y(p, q):
        arrived(acts[p].at[col_at(q) * 4 + x, core], ay_recv.at[p * 4 + col_at(q)])
        acts_x(p, q)

    def acts_core(p, q):
        arrived(acts[p].at[pl.ds(0, 3), core], ax_recv.at[p * 4 + col_at(q)])
        group = acts[p].at[pl.ds(col_at(q) * 4, 4), core]
        remote(group, group, ac_send.at[p], ac_recv.at[p], core_dev).start()

    def acts_all(p):
        arrived(acts[p].at[:, core], ac_recv.at[p])

    z_hi, z_sub = lax.div(z, 4), lax.rem(z, 4)

    def out_start(p):
        for q in FAR + (0,):
            zs = pl.ds(lax.rem(z_hi + q, 4) * 4, 4)
            remote(
                p4.at[p, 1 - y_lo, zs], n_in.at[p, zs], on_send.at[p], on_recv.at[p * 4 + q], next_dev
            ).start()

    def out_z(p, q):
        first = lax.rem(z_hi + q, 4) * 4
        zs = pl.ds(first, 4)
        arrived(n_in.at[p, zs], on_recv.at[p * 4 + q])
        zpack[p, zs] = (p4[p, y_lo, zs] + n_in[p, zs]).astype(BF16)
        for step in FAR + (0,):
            if q or step:
                other = first + lax.rem(z_sub + step, 4)
                remote(
                    zpack.at[p, other], z_in.at[p, z], oz_send.at[p], oz_recv.at[p], z_dev(other)
                ).start()

    def out_all(p):
        arrived(z_in.at[p, pl.ds(0, 15)], oz_recv.at[p])
        total = p4[p, y_lo, z] + n_in[p, z]

        def body(i, total):
            return total + z_in[p, lax.rem(z + i, 16)].astype(F32)

        return lax.fori_loop(1, 16, body, total).astype(BF16)

    gather_start(0)
    gather_start(1)
    gather_pass(0)
    tok_all = gather_all(0)
    for load in loads:
        load.wait()
    part0[:, :, :, 0:ff] = dot(tok_all, gw[...], 1, 0).reshape(16, 2, 8, ff)
    part0[:, :, :, ff:] = dot(tok_all, uw[...], 1, 0).reshape(16, 2, 8, ff)
    sums_start(0)
    gather_pass(1)
    for q in FAR + (0,):
        sums_x(0, q)
    grad_all = gather_all(1)
    part1[...] = dot(grad_all, dw[...], 1, 1).reshape(16, 2, 8, ff)
    sums_start(1)
    for q in FAR:
        sums_y(0, q)
    for q in FAR + (0,):
        sums_x(1, q)
    sums_y(0, 0)
    total = sums_total(0)
    gate_pre = total[:, 0:ff]
    up_proj = total[:, ff:]
    sig = jax.nn.sigmoid(gate_pre)
    acts0[col * 4 + x, core] = (gate_pre * sig * up_proj).astype(BF16)
    acts_start(0)
    for q in FAR + (0,):
        sums_y(1, q)
    for q in NEAR:
        acts_y(0, q)
    d_hidden = sums_total(1)
    acts1[col * 4 + x, core, :, 0:ff] = (
        d_hidden * up_proj * sig * (1.0 + gate_pre * (1.0 - sig))
    ).astype(BF16)
    acts1[col * 4 + x, core, :, ff:] = (d_hidden * gate_pre * sig).astype(BF16)
    acts_start(1)
    for q in (0,) + NEAR:
        acts_core(0, q)
    for q in NEAR:
        acts_y(1, q)
    acts_all(0)
    hid = acts0[...].astype(F32).reshape(256, ff).astype(BF16)
    p4[0] = dot(hid, dw[...], 1, 0).reshape(2, 16, 8, d)
    out_start(0)
    for q in (0,) + NEAR:
        acts_core(1, q)
    for q in FAR + (0,):
        out_z(0, q)
    acts_all(1)
    d_gate = acts1[:, :, :, 0:ff].astype(F32).reshape(256, ff).astype(BF16)
    d_up = acts1[:, :, :, ff:].astype(F32).reshape(256, ff).astype(BF16)
    p4[1] = (dot(d_gate, gw[...], 1, 1) + dot(d_up, uw[...], 1, 1)).reshape(2, 16, 8, d)
    out_start(1)
    gg[...] = dot(tok_all, d_gate, 0, 0).astype(BF16)
    stores = [pltpu.make_async_copy(gg, gg_hbm, store_sem.at[0])]
    stores[0].start()
    for q in FAR + (0,):
        out_z(1, q)
    gu[...] = dot(tok_all, d_up, 0, 0).astype(BF16)
    stores.append(pltpu.make_async_copy(gu, gu_hbm, store_sem.at[1]))
    stores[1].start()
    gd[...] = dot(hid, grad_all, 0, 0).astype(BF16)
    stores.append(pltpu.make_async_copy(gd, gd_hbm, store_sem.at[2]))
    stores[2].start()
    for p in (0, 1):
        left(gath[p].at[pl.ds(0, 15)], tz_send.at[p])
        left(gath[p].at[pl.ds(0, 16)], ty_send.at[p])
        left(core_in[p], sc_send.at[p])
        left(pack[p].at[pl.ds(0, 12)], sx_send.at[p])
        left(y_in[p].at[pl.ds(0, 3)], sy_send.at[p])
        left(acts[p].at[pl.ds(0, 3), core], ay_send.at[p])
        left(acts[p].at[pl.ds(0, 12), core], ax_send.at[p])
        left(acts[p].at[:, core], ac_send.at[p])
        left(n_in.at[p], on_send.at[p])
    lo_ref[...] = out_all(0)
    gt_ref[...] = out_all(1)
    for p in (0, 1):
        left(zpack.at[p, pl.ds(0, 15)], oz_send.at[p])
    for store in stores:
        store.wait()


def land(*refs):
    sources, targets, sem = refs[:5], refs[5:10], refs[10]
    copies = [
        pltpu.make_async_copy(source, target, sem.at[i])
        for i, (source, target) in enumerate(zip(sources, targets))
    ]
    for copy in copies:
        copy.start()
    for copy in copies:
        copy.wait()


def per_device(tokens, grad_out, gate_weight, up_weight, down_weight):
    d, ff = gate_weight.shape
    vmem = pl.BlockSpec(memory_space=pltpu.VMEM)
    hbm = pl.BlockSpec(memory_space=pltpu.HBM)
    dma = pltpu.SemaphoreType.DMA
    pair = (1, 1)
    results = pl.pallas_call(
        kernel,
        out_shape=(
            jax.ShapeDtypeStruct((8, d), BF16),
            jax.ShapeDtypeStruct((8, d), BF16),
            jax.ShapeDtypeStruct((d, ff), BF16),
            jax.ShapeDtypeStruct((d, ff), BF16),
            jax.ShapeDtypeStruct((ff, d), BF16),
        ),
        in_specs=[hbm] * 5,
        out_specs=(vmem, vmem, hbm, hbm, hbm),
        scratch_shapes=[
            pltpu.VMEM((d, ff), BF16),
            pltpu.VMEM((d, ff), BF16),
            pltpu.VMEM((ff, d), BF16),
            pltpu.VMEM((32, 8, d), BF16),
            pltpu.VMEM((32, 8, d), BF16),
            pltpu.VMEM((16, 2, 8, 2 * ff), F32),
            pltpu.VMEM((16, 2, 8, ff), F32),
            pltpu.VMEM((16, 8, 2 * ff), F32),
            pltpu.VMEM((16, 8, ff), F32),
            pltpu.VMEM((16, 8, 2 * ff), BF16),
            pltpu.VMEM((16, 8, ff), BF16),
            pltpu.VMEM((16, 8, 2 * ff), BF16),
            pltpu.VMEM((16, 8, ff), BF16),
            pltpu.VMEM((4, 8, 2 * ff), F32),
            pltpu.VMEM((4, 8, ff), F32),
            pltpu.VMEM((4, 8, 2 * ff), F32),
            pltpu.VMEM((4, 8, ff), F32),
            pltpu.VMEM((16, 2, 8, ff), BF16),
            pltpu.VMEM((16, 2, 8, 2 * ff), BF16),
            pltpu.VMEM((2, 2, 16, 8, d), F32),
            pltpu.VMEM((2, 16, 8, d), F32),
            pltpu.VMEM((2, 16, 8, d), BF16),
            pltpu.VMEM((2, 16, 8, d), BF16),
            pltpu.VMEM((d, ff), BF16),
            pltpu.VMEM((d, ff), BF16),
            pltpu.VMEM((ff, d), BF16),
            dma((5,)), dma((3,)),
            dma((2,)), dma((32,)), dma((2,)), dma((2,)),
            dma((2,)), dma((8,)), dma((2,)), dma((8,)), dma((2,)), dma((2,)),
            dma((2,)), dma((8,)), dma((2,)), dma((8,)), dma((2,)), dma((2,)),
            dma((2,)), dma((8,)), dma((2,)), dma((2,)),
        ],
        compiler_params=pltpu.CompilerParams(
            collective_id=0, has_side_effects=True, vmem_limit_bytes=62 << 20
        ),
        name="swiglu_exchange",
    )(tokens, grad_out, gate_weight, up_weight, down_weight)
    return pl.pallas_call(
        land,
        out_shape=tuple(jax.ShapeDtypeStruct(r.shape, r.dtype) for r in results),
        in_specs=[pl.BlockSpec(memory_space=pl.ANY)] * 5,
        out_specs=(pl.BlockSpec(memory_space=pl.ANY),) * 5,
        scratch_shapes=[dma((5,))],
        name="land",
    )(*results)


def solution(mesh):
    acts = P("row", ("col", "depth"))
    weights = P(("col", "depth"), "row")
    return jax.shard_map(
        per_device,
        mesh=mesh,
        in_specs=(acts, acts, weights, weights, acts),
        out_specs=(acts, acts, weights, weights, acts),
        check_vma=False,
    )
```

```python
import functools
import jax
import jax.numpy as jnp
from jax import lax
from jax.experimental import pallas as pl
from jax.experimental.pallas import tpu as pltpu
from jax.sharding import PartitionSpec as P

MESH = pl.DeviceIdType.MESH
F32 = jnp.float32
BF16 = jnp.bfloat16
FAR = (2, 1, 3)
NEAR = (1, 3, 2)


def dot(left, right, left_dim, right_dim):
    return lax.dot_general(
        left, right, (((left_dim,), (right_dim,)), ((), ())), preferred_element_type=F32
    )


def kernel(
    tok_hbm, grad_hbm, gw_hbm, uw_hbm, dw_hbm,
    lo_ref, gt_ref, gg_hbm, gu_hbm, gd_hbm,
    gw, uw, dw, gath0, gath1,
    part0, part1, core_in0, core_in1, pack0, pack1, x_in0, x_in1, y_out0, y_out1, y_in0, y_in1,
    acts0, acts1, p4, n_in, zpack, z_in, gg, gu, gd,
    load_sem, store_sem,
    tz_send, tz_recv, ty_send, ty_recv,
    sc_send, sc_recv, sx_send, sx_recv, sy_send, sy_recv,
    ay_send, ay_recv, ax_send, ax_recv, ac_send, ac_recv,
    on_send, on_recv, oz_send, oz_recv,
):
    row, col, depth = lax.axis_index("row"), lax.axis_index("col"), lax.axis_index("depth")
    y_lo, z = lax.div(row, 16), lax.rem(row, 16)
    x, core = lax.div(depth, 2), lax.rem(depth, 2)
    d, ff = gw.shape
    gath = (gath0, gath1)
    part, core_in, pack = (part0, part1), (core_in0, core_in1), (pack0, pack1)
    x_in, y_out, y_in, acts = (x_in0, x_in1), (y_out0, y_out1), (y_in0, y_in1), (acts0, acts1)

    def z_dev(other):
        return (y_lo * 16 + other, col, depth)

    def col_dev(other):
        return (row, other, depth)

    def x_dev(other):
        return (row, col, other * 2 + core)

    next_dev = ((1 - y_lo) * 16 + z, col, depth)
    core_dev = (row, col, x * 2 + 1 - core)

    def remote(src, dst, send, recv, device):
        return pltpu.make_async_remote_copy(
            src_ref=src, dst_ref=dst, send_sem=send, recv_sem=recv,
            device_id=device, device_id_type=MESH,
        )

    def arrived(ref, recv):
        remote(ref, ref, load_sem.at[0], recv, core_dev).wait_recv()

    def left(ref, send):
        remote(ref, ref, send, load_sem.at[0], core_dev).wait_send()

    def z_off(i):
        return 8 + lax.div(i + 1, 2) * (2 * lax.rem(i, 2) - 1)

    def col_at(q):
        return lax.rem(col + q, 4)

    def x_at(step):
        return lax.rem(x + step, 4)

    own_loads = [
        pltpu.make_async_copy(tok_hbm, gath0.at[row], load_sem.at[0]),
        pltpu.make_async_copy(grad_hbm, gath1.at[row], load_sem.at[1]),
    ]
    loads = [
        pltpu.make_async_copy(gw_hbm, gw, load_sem.at[2]),
        pltpu.make_async_copy(uw_hbm, uw, load_sem.at[3]),
        pltpu.make_async_copy(dw_hbm, dw, load_sem.at[4]),
    ]
    for load in own_loads + loads:
        load.start()

    barrier = pltpu.get_barrier_semaphore()

    def greet(device):
        pl.semaphore_signal(barrier, inc=1, device_id=device, device_id_type=MESH)

    def greet_z(i, c):
        greet(z_dev(lax.rem(z + z_off(i), 16)))
        return c

    lax.fori_loop(0, 15, greet_z, 0)
    for step in FAR:
        greet(col_dev(col_at(step)))
        greet(x_dev(x_at(step)))
    greet(next_dev)
    greet(core_dev)
    for load in own_loads:
        load.wait()
    pl.semaphore_wait(barrier, 23)

    def pass_on(p, src_z):
        slot = gath[p].at[y_lo * 16 + src_z]
        remote(slot, slot, ty_send.at[p], ty_recv.at[p], next_dev).start()

    def gather_start(p):
        def body(i, c):
            slot = gath[p].at[row]
            remote(slot, slot, tz_send.at[p], tz_recv.at[p * 16 + z], z_dev(lax.rem(z + z_off(i), 16))).start()
            return c
        lax.fori_loop(0, 15, body, 0)
        pass_on(p, z)

    def gather_pass(p):
        def body(k, c):
            src_z = lax.rem(z + 16 - z_off(14 - k), 16)
            arrived(gath[p].at[y_lo * 16 + src_z], tz_recv.at[p * 16 + src_z])
            pass_on(p, src_z)
            return c
        lax.fori_loop(0, 15, body, 0)

    def gather_all(p):
        arrived(gath[p].at[pl.ds((1 - y_lo) * 16, 16)], ty_recv.at[p])
        return gath[p][...].astype(F32).reshape(256, d).astype(BF16)

    def sums_start(p):
        for q in FAR + (0,):
            chips = pl.ds(col_at(q) * 4, 4)
            remote(
                part[p].at[chips, 1 - core], core_in[p].at[chips],
                sc_send.at[p], sc_recv.at[p * 4 + q], core_dev,
            ).start()

    def sums_x(p, q):
        first = col_at(q) * 4
        chips = pl.ds(first, 4)
        arrived(core_in[p].at[chips], sc_recv.at[p * 4 + q])
        pack[p][chips] = (part[p][chips, core] + core_in[p][chips]).astype(BF16)
        for step in FAR:
            remote(
                pack[p].at[first + x_at(step)], x_in[p].at[first + x],
                sx_send.at[p], sx_recv.at[p * 4 + col_at(q)], x_dev(x_at(step)),
            ).start()

    def sums_y(p, q):
        first = col_at(q) * 4
        arrived(x_in[p].at[pl.ds(0, 3)], sx_recv.at[p * 4 + col_at(q)])
        total = part[p][first + x, core] + core_in[p][first + x]
        for step in FAR:
            total = total + x_in[p][first + x_at(step)].astype(F32)
        y_out[p][col_at(q)] = total
        if q:
            remote(
                y_out[p].at[col_at(q)], y_in[p].at[col], sy_send.at[p], sy_recv.at[p], col_dev(col_at(q))
            ).start()

    def sums_total(p):
        arrived(y_in[p].at[pl.ds(0, 3)], sy_recv.at[p])
        total = y_out[p][col]
        for q in FAR:
            total = total + y_in[p][col_at(q)]
        return total

    def acts_x(p, q):
        slot = acts[p].at[col_at(q) * 4 + x, core]
        for step in FAR:
            remote(
                slot, slot, ax_send.at[p], ax_recv.at[p * 4 + col_at(q)], x_dev(x_at(step))
            ).start()

    def acts_start(p):
        slot = acts[p].at[col * 4 + x, core]
        for q in FAR:
            remote(slot, slot, ay_send.at[p], ay_recv.at[p * 4 + col], col_dev(col_at(q))).start()
        acts_x(p, 0)

    def acts_y(p, q):
        arrived(acts[p].at[col_at(q) * 4 + x, core], ay_recv.at[p * 4 + col_at(q)])
        acts_x(p, q)

    def acts_core(p, q):
        arrived(acts[p].at[pl.ds(0, 3), core], ax_recv.at[p * 4 + col_at(q)])
        group = acts[p].at[pl.ds(col_at(q) * 4, 4), core]
        remote(group, group, ac_send.at[p], ac_recv.at[p], core_dev).start()

    def acts_all(p):
        arrived(acts[p].at[:, core], ac_recv.at[p])

    z_hi, z_sub = lax.div(z, 4), lax.rem(z, 4)

    def out_start(p):
        for q in FAR + (0,):
            zs = pl.ds(lax.rem(z_hi + q, 4) * 4, 4)
            remote(
                p4.at[p, 1 - y_lo, zs], n_in.at[p, zs], on_send.at[p], on_recv.at[p * 4 + q], next_dev
            ).start()

    def out_z(p, q):
        first = lax.rem(z_hi + q, 4) * 4
        zs = pl.ds(first, 4)
        arrived(n_in.at[p, zs], on_recv.at[p * 4 + q])
        zpack[p, zs] = (p4[p, y_lo, zs] + n_in[p, zs]).astype(BF16)
        for step in FAR + (0,):
            if q or step:
                other = first + lax.rem(z_sub + step, 4)
                remote(
                    zpack.at[p, other], z_in.at[p, z], oz_send.at[p], oz_recv.at[p], z_dev(other)
                ).start()

    def out_all(p):
        arrived(z_in.at[p, pl.ds(0, 15)], oz_recv.at[p])
        total = p4[p, y_lo, z] + n_in[p, z]

        def body(i, total):
            return total + z_in[p, lax.rem(z + i, 16)].astype(F32)

        return lax.fori_loop(1, 16, body, total).astype(BF16)

    gather_start(0)
    gather_start(1)
    gather_pass(0)
    tok_all = gather_all(0)
    for load in loads:
        load.wait()
    part0[:, :, :, 0:ff] = dot(tok_all, gw[...], 1, 0).reshape(16, 2, 8, ff)
    part0[:, :, :, ff:] = dot(tok_all, uw[...], 1, 0).reshape(16, 2, 8, ff)
    sums_start(0)
    gather_pass(1)
    for q in FAR + (0,):
        sums_x(0, q)
    grad_all = gather_all(1)
    part1[...] = dot(grad_all, dw[...], 1, 1).reshape(16, 2, 8, ff)
    sums_start(1)
    for q in FAR:
        sums_y(0, q)
    for q in FAR + (0,):
        sums_x(1, q)
    sums_y(0, 0)
    total = sums_total(0)
    gate_pre = total[:, 0:ff]
    up_proj = total[:, ff:]
    sig = jax.nn.sigmoid(gate_pre)
    acts0[col * 4 + x, core] = (gate_pre * sig * up_proj).astype(BF16)
    acts_start(0)
    for q in FAR + (0,):
        sums_y(1, q)
    for q in NEAR:
        acts_y(0, q)
    d_hidden = sums_total(1)
    acts1[col * 4 + x, core, :, 0:ff] = (
        d_hidden * up_proj * sig * (1.0 + gate_pre * (1.0 - sig))
    ).astype(BF16)
    acts1[col * 4 + x, core, :, ff:] = (d_hidden * gate_pre * sig).astype(BF16)
    acts_start(1)
    for q in (0,) + NEAR:
        acts_core(0, q)
    for q in NEAR:
        acts_y(1, q)
    acts_all(0)
    hid = acts0[...].astype(F32).reshape(256, ff).astype(BF16)
    p4[0] = dot(hid, dw[...], 1, 0).reshape(2, 16, 8, d)
    out_start(0)
    for q in (0,) + NEAR:
        acts_core(1, q)
    for q in FAR + (0,):
        out_z(0, q)
    acts_all(1)
    d_gate = acts1[:, :, :, 0:ff].astype(F32).reshape(256, ff).astype(BF16)
    d_up = acts1[:, :, :, ff:].astype(F32).reshape(256, ff).astype(BF16)
    p4[1] = (dot(d_gate, gw[...], 1, 1) + dot(d_up, uw[...], 1, 1)).reshape(2, 16, 8, d)
    out_start(1)
    gg[...] = dot(tok_all, d_gate, 0, 0).astype(BF16)
    stores = [pltpu.make_async_copy(gg, gg_hbm, store_sem.at[0])]
    stores[0].start()
    for q in FAR + (0,):
        out_z(1, q)
    gu[...] = dot(tok_all, d_up, 0, 0).astype(BF16)
    stores.append(pltpu.make_async_copy(gu, gu_hbm, store_sem.at[1]))
    stores[1].start()
    gd[...] = dot(hid, grad_all, 0, 0).astype(BF16)
    stores.append(pltpu.make_async_copy(gd, gd_hbm, store_sem.at[2]))
    stores[2].start()
    for p in (0, 1):
        left(gath[p].at[pl.ds(0, 15)], tz_send.at[p])
        left(gath[p].at[pl.ds(0, 16)], ty_send.at[p])
        left(core_in[p], sc_send.at[p])
        left(pack[p].at[pl.ds(0, 12)], sx_send.at[p])
        left(y_in[p].at[pl.ds(0, 3)], sy_send.at[p])
        left(acts[p].at[pl.ds(0, 3), core], ay_send.at[p])
        left(acts[p].at[pl.ds(0, 12), core], ax_send.at[p])
        left(acts[p].at[:, core], ac_send.at[p])
        left(n_in.at[p], on_send.at[p])
    lo_ref[...] = out_all(0)
    gt_ref[...] = out_all(1)
    for p in (0, 1):
        left(zpack.at[p, pl.ds(0, 15)], oz_send.at[p])
    for store in stores:
        store.wait()


def land(*refs):
    sources, targets, held = refs[:5], refs[5:10], refs[10:15]
    in_sem, out_sem = refs[15:]
    loads = [
        pltpu.make_async_copy(source, buf, in_sem.at[i])
        for i, (source, buf) in enumerate(zip(sources, held))
    ]
    stores = [
        pltpu.make_async_copy(buf, target, out_sem.at[i])
        for i, (buf, target) in enumerate(zip(held, targets))
    ]
    for load in loads:
        load.start()
    for load, store in zip(loads, stores):
        load.wait()
        store.start()
    for store in stores:
        store.wait()


def per_device(tokens, grad_out, gate_weight, up_weight, down_weight):
    d, ff = gate_weight.shape
    vmem = pl.BlockSpec(memory_space=pltpu.VMEM)
    hbm = pl.BlockSpec(memory_space=pltpu.HBM)
    dma = pltpu.SemaphoreType.DMA
    pair = (1, 1)
    results = pl.pallas_call(
        kernel,
        out_shape=(
            jax.ShapeDtypeStruct((8, d), BF16),
            jax.ShapeDtypeStruct((8, d), BF16),
            jax.ShapeDtypeStruct((d, ff), BF16),
            jax.ShapeDtypeStruct((d, ff), BF16),
            jax.ShapeDtypeStruct((ff, d), BF16),
        ),
        in_specs=[hbm] * 5,
        out_specs=(vmem, vmem, hbm, hbm, hbm),
        scratch_shapes=[
            pltpu.VMEM((d, ff), BF16),
            pltpu.VMEM((d, ff), BF16),
            pltpu.VMEM((ff, d), BF16),
            pltpu.VMEM((32, 8, d), BF16),
            pltpu.VMEM((32, 8, d), BF16),
            pltpu.VMEM((16, 2, 8, 2 * ff), F32),
            pltpu.VMEM((16, 2, 8, ff), F32),
            pltpu.VMEM((16, 8, 2 * ff), F32),
            pltpu.VMEM((16, 8, ff), F32),
            pltpu.VMEM((16, 8, 2 * ff), BF16),
            pltpu.VMEM((16, 8, ff), BF16),
            pltpu.VMEM((16, 8, 2 * ff), BF16),
            pltpu.VMEM((16, 8, ff), BF16),
            pltpu.VMEM((4, 8, 2 * ff), F32),
            pltpu.VMEM((4, 8, ff), F32),
            pltpu.VMEM((4, 8, 2 * ff), F32),
            pltpu.VMEM((4, 8, ff), F32),
            pltpu.VMEM((16, 2, 8, ff), BF16),
            pltpu.VMEM((16, 2, 8, 2 * ff), BF16),
            pltpu.VMEM((2, 2, 16, 8, d), F32),
            pltpu.VMEM((2, 16, 8, d), F32),
            pltpu.VMEM((2, 16, 8, d), BF16),
            pltpu.VMEM((2, 16, 8, d), BF16),
            pltpu.VMEM((d, ff), BF16),
            pltpu.VMEM((d, ff), BF16),
            pltpu.VMEM((ff, d), BF16),
            dma((5,)), dma((3,)),
            dma((2,)), dma((32,)), dma((2,)), dma((2,)),
            dma((2,)), dma((8,)), dma((2,)), dma((8,)), dma((2,)), dma((2,)),
            dma((2,)), dma((8,)), dma((2,)), dma((8,)), dma((2,)), dma((2,)),
            dma((2,)), dma((8,)), dma((2,)), dma((2,)),
        ],
        compiler_params=pltpu.CompilerParams(
            collective_id=0, has_side_effects=True, vmem_limit_bytes=62 << 20
        ),
        name="swiglu_exchange",
    )(tokens, grad_out, gate_weight, up_weight, down_weight)
    return pl.pallas_call(
        land,
        out_shape=tuple(jax.ShapeDtypeStruct(r.shape, r.dtype) for r in results),
        in_specs=[pl.BlockSpec(memory_space=pl.ANY)] * 5,
        out_specs=(pl.BlockSpec(memory_space=pl.ANY),) * 5,
        scratch_shapes=[pltpu.VMEM(r.shape, r.dtype) for r in results] + [dma((5,)), dma((5,))],
        name="land",
    )(*results)


def solution(mesh):
    acts = P("row", ("col", "depth"))
    weights = P(("col", "depth"), "row")
    return jax.shard_map(
        per_device,
        mesh=mesh,
        in_specs=(acts, acts, weights, weights, acts),
        out_specs=(acts, acts, weights, weights, acts),
        check_vma=False,
    )
```

```python
import functools
import jax
import jax.numpy as jnp
from jax import lax
from jax.experimental import pallas as pl
from jax.experimental.pallas import tpu as pltpu
from jax.sharding import PartitionSpec as P

MESH = pl.DeviceIdType.MESH
F32 = jnp.float32
BF16 = jnp.bfloat16
FAR = (2, 1, 3)
NEAR = (1, 3, 2)
Z_NEAR = (12, 4, 13, 3, 14, 2, 15, 1)
Z_FAR = (11, 5, 10, 6, 9, 7, 8)


def dot(left, right, left_dim, right_dim):
    return lax.dot_general(
        left, right, (((left_dim,), (right_dim,)), ((), ())), preferred_element_type=F32
    )


def kernel(
    tok_hbm, grad_hbm, gw_hbm, uw_hbm, dw_hbm,
    lo_ref, gt_ref, gg_hbm, gu_hbm, gd_hbm,
    gw, uw, dw, gath0, gath1,
    part0, part1, core_in0, core_in1, pack0, pack1, x_in0, x_in1, y_out0, y_out1, y_in0, y_in1,
    far_out0, far_out1, far_in0, far_in1, acts0, acts1, p4, n_in, zpack, z_in, gg, gu, gd,
    load_sem, store_sem,
    tz_send, tz_recv, ty_send, ty_recv,
    sc_send, sc_recv, sx_send, sx_recv, sy_send, sy_recv, sf_send, sf_recv,
    ay_send, ay_recv, ax_send, ax_recv, ac_send, ac_recv,
    on_send, on_recv, oz_send, oz_recv,
):
    row, col, depth = lax.axis_index("row"), lax.axis_index("col"), lax.axis_index("depth")
    y_lo, z = lax.div(row, 16), lax.rem(row, 16)
    x, core = lax.div(depth, 2), lax.rem(depth, 2)
    d, ff = gw.shape
    gath = (gath0, gath1)
    far_out, far_in = (far_out0, far_out1), (far_in0, far_in1)
    part, core_in, pack = (part0, part1), (core_in0, core_in1), (pack0, pack1)
    x_in, y_out, y_in, acts = (x_in0, x_in1), (y_out0, y_out1), (y_in0, y_in1), (acts0, acts1)

    def z_dev(other):
        return (y_lo * 16 + other, col, depth)

    def col_dev(other):
        return (row, other, depth)

    def x_dev(other):
        return (row, col, other * 2 + core)

    next_dev = ((1 - y_lo) * 16 + z, col, depth)
    core_dev = (row, col, x * 2 + 1 - core)

    def remote(src, dst, send, recv, device):
        return pltpu.make_async_remote_copy(
            src_ref=src, dst_ref=dst, send_sem=send, recv_sem=recv,
            device_id=device, device_id_type=MESH,
        )

    def arrived(ref, recv):
        remote(ref, ref, load_sem.at[0], recv, core_dev).wait_recv()

    def left(ref, send):
        remote(ref, ref, send, load_sem.at[0], core_dev).wait_send()

    def col_at(q):
        return lax.rem(col + q, 4)

    def x_at(step):
        return lax.rem(x + step, 4)

    own_loads = [
        pltpu.make_async_copy(tok_hbm, gath0.at[row], load_sem.at[0]),
        pltpu.make_async_copy(grad_hbm, gath1.at[row], load_sem.at[1]),
    ]
    loads = [
        pltpu.make_async_copy(gw_hbm, gw, load_sem.at[2]),
        pltpu.make_async_copy(uw_hbm, uw, load_sem.at[3]),
        pltpu.make_async_copy(dw_hbm, dw, load_sem.at[4]),
    ]
    for load in own_loads + loads:
        load.start()

    barrier = pltpu.get_barrier_semaphore()

    def greet(device):
        pl.semaphore_signal(barrier, inc=1, device_id=device, device_id_type=MESH)

    for off in Z_NEAR:
        greet(z_dev(lax.rem(z + off, 16)))
    for step in FAR:
        greet(col_dev(col_at(step)))
        greet(x_dev(x_at(step)))
    greet(next_dev)
    greet(core_dev)
    for load in own_loads:
        load.wait()
    pl.semaphore_wait(barrier, 16)

    def pass_on(p, src_z):
        slot = gath[p].at[y_lo * 16 + src_z]
        remote(slot, slot, ty_send.at[p], ty_recv.at[p], next_dev).start()

    def gather_start(p):
        slot = gath[p].at[row]
        for off in Z_NEAR:
            remote(
                slot, slot, tz_send.at[p], tz_recv.at[p * 16 + z], z_dev(lax.rem(z + off, 16))
            ).start()
        pass_on(p, z)

    def gather_pass(p, offs):
        for off in offs:
            src_z = lax.rem(z + off, 16)
            slot = gath[p].at[y_lo * 16 + src_z]
            arrived(slot, tz_recv.at[p * 16 + src_z])
            if off in (12, 13, 14, 15) or off in (1, 2, 3):
                onward = 4 if off > 8 else 12
                remote(
                    slot, slot, tz_send.at[p], tz_recv.at[p * 16 + src_z], z_dev(lax.rem(z + onward, 16))
                ).start()
            pass_on(p, src_z)

    def gather_all(p):
        arrived(gath[p].at[pl.ds((1 - y_lo) * 16, 16)], ty_recv.at[p])
        return gath[p][...].astype(F32).reshape(256, d).astype(BF16)

    def col_of(j):
        return lax.rem(2 * y_lo + j, 4)

    def sums_start(p, j):
        chips = pl.ds(col_of(j) * 4, 4)
        remote(
            part[p].at[chips, 1 - core], core_in[p].at[chips],
            sc_send.at[p], sc_recv.at[p * 4 + j], core_dev,
        ).start()

    def sums_x(p, j):
        first = col_of(j) * 4
        chips = pl.ds(first, 4)
        arrived(core_in[p].at[chips], sc_recv.at[p * 4 + j])
        pack[p][chips] = (part[p][chips, core] + core_in[p][chips]).astype(BF16)
        for step in FAR:
            remote(
                pack[p].at[first + x_at(step)], x_in[p].at[first + x],
                sx_send.at[p], sx_recv.at[p * 4 + j], x_dev(x_at(step)),
            ).start()

    def sums_y(p, j):
        to = col_of(j)
        first = to * 4
        arrived(x_in[p].at[pl.ds(0, 3)], sx_recv.at[p * 4 + j])
        total = part[p][first + x, core] + core_in[p][first + x]
        for step in FAR:
            total = total + x_in[p][first + x_at(step)].astype(F32)
        y_out[p][to] = total
        away = lax.rem(to + 4 - col, 4)

        @pl.when(away == 2)
        def _():
            far_out[p][...] = total.astype(BF16)
            remote(far_out[p], far_in[p], sf_send.at[p], sf_recv.at[p], col_dev(to)).start()

        @pl.when(lax.rem(away, 2) == 1)
        def _():
            remote(y_out[p].at[to], y_in[p].at[col], sy_send.at[p], sy_recv.at[p], col_dev(to)).start()

    def sums_total(p):
        arrived(y_in[p].at[pl.ds(0, 2)], sy_recv.at[p])
        total = y_out[p][col] + y_in[p][col_at(1)] + y_in[p][col_at(3)]
        arrived(far_in[p], sf_recv.at[p])
        return total + far_in[p][...].astype(F32)

    def acts_x(p, q):
        slot = acts[p].at[col_at(q) * 4 + x, core]
        for step in FAR:
            remote(
                slot, slot, ax_send.at[p], ax_recv.at[p * 4 + col_at(q)], x_dev(x_at(step))
            ).start()

    def acts_start(p):
        slot = acts[p].at[col * 4 + x, core]
        for q in FAR:
            remote(slot, slot, ay_send.at[p], ay_recv.at[p * 4 + col], col_dev(col_at(q))).start()
        acts_x(p, 0)

    def acts_y(p, q):
        arrived(acts[p].at[col_at(q) * 4 + x, core], ay_recv.at[p * 4 + col_at(q)])
        acts_x(p, q)

    def acts_core(p, q):
        arrived(acts[p].at[pl.ds(0, 3), core], ax_recv.at[p * 4 + col_at(q)])
        group = acts[p].at[pl.ds(col_at(q) * 4, 4), core]
        remote(group, group, ac_send.at[p], ac_recv.at[p], core_dev).start()

    def acts_all(p):
        arrived(acts[p].at[:, core], ac_recv.at[p])

    z_hi, z_sub = lax.div(z, 4), lax.rem(z, 4)

    def out_start(p):
        for q in FAR + (0,):
            zs = pl.ds(lax.rem(z_hi + q, 4) * 4, 4)
            remote(
                p4.at[p, 1 - y_lo, zs], n_in.at[p, zs], on_send.at[p], on_recv.at[p * 4 + q], next_dev
            ).start()

    def out_z(p, q):
        first = lax.rem(z_hi + q, 4) * 4
        zs = pl.ds(first, 4)
        arrived(n_in.at[p, zs], on_recv.at[p * 4 + q])
        zpack[p, zs] = (p4[p, y_lo, zs] + n_in[p, zs]).astype(BF16)
        for step in FAR + (0,):
            if q or step:
                other = first + lax.rem(z_sub + step, 4)
                remote(
                    zpack.at[p, other], z_in.at[p, z], oz_send.at[p], oz_recv.at[p], z_dev(other)
                ).start()

    def out_all(p):
        arrived(z_in.at[p, pl.ds(0, 15)], oz_recv.at[p])
        total = p4[p, y_lo, z] + n_in[p, z]

        def body(i, total):
            return total + z_in[p, lax.rem(z + i, 16)].astype(F32)

        return lax.fori_loop(1, 16, body, total).astype(BF16)

    gather_start(0)
    gather_start(1)
    gather_pass(0, Z_NEAR[::-1])
    gather_pass(1, Z_NEAR[::-1])
    gather_pass(0, Z_FAR)
    for load in loads:
        load.wait()

    def gate_up(half):
        tok = gath0[pl.ds(half * 16, 16)].astype(F32).reshape(128, d).astype(BF16)
        chips = pl.ds(half * 8, 8)
        part0[chips, :, :, 0:ff] = dot(tok, gw[...], 1, 0).reshape(8, 2, 8, ff)
        part0[chips, :, :, ff:] = dot(tok, uw[...], 1, 0).reshape(8, 2, 8, ff)

    gate_up(y_lo)
    sums_start(0, 0)
    sums_start(0, 1)
    gather_pass(1, Z_FAR)
    sums_x(0, 0)
    sums_x(0, 1)
    tok_all = gather_all(0)
    gate_up(1 - y_lo)
    sums_start(0, 2)
    sums_start(0, 3)
    grad_all = gather_all(1)
    part1[...] = dot(grad_all, dw[...], 1, 1).reshape(16, 2, 8, ff)
    sums_x(0, 2)
    sums_x(0, 3)
    for j in range(4):
        sums_start(1, j)
    sums_y(0, 0)
    sums_y(0, 1)
    sums_x(1, 0)
    sums_x(1, 1)
    sums_y(0, 2)
    sums_x(1, 2)
    sums_x(1, 3)
    sums_y(0, 3)
    total = sums_total(0)
    gate_pre = total[:, 0:ff]
    up_proj = total[:, ff:]
    sig = jax.nn.sigmoid(gate_pre)
    acts0[col * 4 + x, core] = (gate_pre * sig * up_proj).astype(BF16)
    acts_start(0)
    for j in range(4):
        sums_y(1, j)
    for q in NEAR:
        acts_y(0, q)
    d_hidden = sums_total(1)
    acts1[col * 4 + x, core, :, 0:ff] = (
        d_hidden * up_proj * sig * (1.0 + gate_pre * (1.0 - sig))
    ).astype(BF16)
    acts1[col * 4 + x, core, :, ff:] = (d_hidden * gate_pre * sig).astype(BF16)
    acts_start(1)
    for q in (0,) + NEAR:
        acts_core(0, q)
    for q in NEAR:
        acts_y(1, q)
    acts_all(0)
    def out_terms(p, half):
        rows = acts[p][pl.ds(half * 8, 8)].astype(F32)
        if p == 0:
            term = dot(rows.reshape(128, ff).astype(BF16), dw[...], 1, 0)
        else:
            term = dot(rows[:, :, :, 0:ff].reshape(128, ff).astype(BF16), gw[...], 1, 1) + dot(
                rows[:, :, :, ff:].reshape(128, ff).astype(BF16), uw[...], 1, 1
            )
        p4[p, half] = term.reshape(16, 8, d)

    out_terms(0, 1 - y_lo)
    out_start(0)
    out_terms(0, y_lo)
    hid = acts0[...].astype(F32).reshape(256, ff).astype(BF16)
    for q in (0,) + NEAR:
        acts_core(1, q)
    for q in FAR + (0,):
        out_z(0, q)
    acts_all(1)
    out_terms(1, 1 - y_lo)
    out_start(1)
    out_terms(1, y_lo)
    d_gate = acts1[:, :, :, 0:ff].astype(F32).reshape(256, ff).astype(BF16)
    d_up = acts1[:, :, :, ff:].astype(F32).reshape(256, ff).astype(BF16)
    for q in FAR + (0,):
        out_z(1, q)
    gg[...] = dot(tok_all, d_gate, 0, 0).astype(BF16)
    stores = [pltpu.make_async_copy(gg, gg_hbm, store_sem.at[0])]
    stores[0].start()
    gu[...] = dot(tok_all, d_up, 0, 0).astype(BF16)
    stores.append(pltpu.make_async_copy(gu, gu_hbm, store_sem.at[1]))
    stores[1].start()
    gd[...] = dot(hid, grad_all, 0, 0).astype(BF16)
    stores.append(pltpu.make_async_copy(gd, gd_hbm, store_sem.at[2]))
    stores[2].start()
    for p in (0, 1):
        left(gath[p].at[pl.ds(0, 15)], tz_send.at[p])
        left(gath[p].at[pl.ds(0, 16)], ty_send.at[p])
        left(core_in[p], sc_send.at[p])
        left(pack[p].at[pl.ds(0, 12)], sx_send.at[p])
        left(y_in[p].at[pl.ds(0, 2)], sy_send.at[p])
        left(far_in[p], sf_send.at[p])
        left(acts[p].at[pl.ds(0, 3), core], ay_send.at[p])
        left(acts[p].at[pl.ds(0, 12), core], ax_send.at[p])
        left(acts[p].at[:, core], ac_send.at[p])
        left(n_in.at[p], on_send.at[p])
    lo_ref[...] = out_all(0)
    gt_ref[...] = out_all(1)
    for p in (0, 1):
        left(zpack.at[p, pl.ds(0, 15)], oz_send.at[p])
    for store in stores:
        store.wait()


def land(*refs):
    sources, targets, held = refs[:5], refs[5:10], refs[10:15]
    in_sem, out_sem = refs[15:]
    loads = [
        pltpu.make_async_copy(source, buf, in_sem.at[i])
        for i, (source, buf) in enumerate(zip(sources, held))
    ]
    stores = [
        pltpu.make_async_copy(buf, target, out_sem.at[i])
        for i, (buf, target) in enumerate(zip(held, targets))
    ]
    for load in loads:
        load.start()
    for load, store in zip(loads, stores):
        load.wait()
        store.start()
    for store in stores:
        store.wait()


def per_device(tokens, grad_out, gate_weight, up_weight, down_weight):
    d, ff = gate_weight.shape
    vmem = pl.BlockSpec(memory_space=pltpu.VMEM)
    hbm = pl.BlockSpec(memory_space=pltpu.HBM)
    dma = pltpu.SemaphoreType.DMA
    results = pl.pallas_call(
        kernel,
        out_shape=(
            jax.ShapeDtypeStruct((8, d), BF16),
            jax.ShapeDtypeStruct((8, d), BF16),
            jax.ShapeDtypeStruct((d, ff), BF16),
            jax.ShapeDtypeStruct((d, ff), BF16),
            jax.ShapeDtypeStruct((ff, d), BF16),
        ),
        in_specs=[hbm] * 5,
        out_specs=(vmem, vmem, hbm, hbm, hbm),
        scratch_shapes=[
            pltpu.VMEM((d, ff), BF16),
            pltpu.VMEM((d, ff), BF16),
            pltpu.VMEM((ff, d), BF16),
            pltpu.VMEM((32, 8, d), BF16),
            pltpu.VMEM((32, 8, d), BF16),
            pltpu.VMEM((16, 2, 8, 2 * ff), F32),
            pltpu.VMEM((16, 2, 8, ff), F32),
            pltpu.VMEM((16, 8, 2 * ff), F32),
            pltpu.VMEM((16, 8, ff), F32),
            pltpu.VMEM((16, 8, 2 * ff), BF16),
            pltpu.VMEM((16, 8, ff), BF16),
            pltpu.VMEM((16, 8, 2 * ff), BF16),
            pltpu.VMEM((16, 8, ff), BF16),
            pltpu.VMEM((4, 8, 2 * ff), F32),
            pltpu.VMEM((4, 8, ff), F32),
            pltpu.VMEM((4, 8, 2 * ff), F32),
            pltpu.VMEM((4, 8, ff), F32),
            pltpu.VMEM((8, 2 * ff), BF16),
            pltpu.VMEM((8, ff), BF16),
            pltpu.VMEM((8, 2 * ff), BF16),
            pltpu.VMEM((8, ff), BF16),
            pltpu.VMEM((16, 2, 8, ff), BF16),
            pltpu.VMEM((16, 2, 8, 2 * ff), BF16),
            pltpu.VMEM((2, 2, 16, 8, d), F32),
            pltpu.VMEM((2, 16, 8, d), F32),
            pltpu.VMEM((2, 16, 8, d), BF16),
            pltpu.VMEM((2, 16, 8, d), BF16),
            pltpu.VMEM((d, ff), BF16),
            pltpu.VMEM((d, ff), BF16),
            pltpu.VMEM((ff, d), BF16),
            dma((5,)), dma((3,)),
            dma((2,)), dma((32,)), dma((2,)), dma((2,)),
            dma((2,)), dma((8,)), dma((2,)), dma((8,)), dma((2,)), dma((2,)), dma((2,)), dma((2,)),
            dma((2,)), dma((8,)), dma((2,)), dma((8,)), dma((2,)), dma((2,)),
            dma((2,)), dma((8,)), dma((2,)), dma((2,)),
        ],
        compiler_params=pltpu.CompilerParams(
            collective_id=0, has_side_effects=True, vmem_limit_bytes=62 << 20
        ),
        name="swiglu_exchange",
    )(tokens, grad_out, gate_weight, up_weight, down_weight)
    return pl.pallas_call(
        land,
        out_shape=tuple(jax.ShapeDtypeStruct(r.shape, r.dtype) for r in results),
        in_specs=[pl.BlockSpec(memory_space=pl.ANY)] * 5,
        out_specs=(pl.BlockSpec(memory_space=pl.ANY),) * 5,
        scratch_shapes=[pltpu.VMEM(r.shape, r.dtype) for r in results] + [dma((5,)), dma((5,))],
        name="land",
    )(*results)


def solution(mesh):
    acts = P("row", ("col", "depth"))
    weights = P(("col", "depth"), "row")
    return jax.shard_map(
        per_device,
        mesh=mesh,
        in_specs=(acts, acts, weights, weights, acts),
        out_specs=(acts, acts, weights, weights, acts),
        check_vma=False,
    )
```

```python
import functools
import jax
import jax.numpy as jnp
from jax import lax
from jax.experimental import pallas as pl
from jax.experimental.pallas import tpu as pltpu
from jax.sharding import PartitionSpec as P

MESH = pl.DeviceIdType.MESH
F32 = jnp.float32
BF16 = jnp.bfloat16
FAR = (2, 1, 3)
NEAR = (1, 3, 2)
Z_NEAR = (12, 4, 13, 3, 14, 2, 15, 1)
Z_FAR = (11, 5, 10, 6, 9, 7, 8)


def dot(left, right, left_dim, right_dim):
    return lax.dot_general(
        left, right, (((left_dim,), (right_dim,)), ((), ())), preferred_element_type=F32
    )


def kernel(
    tok_hbm, grad_hbm, gw_hbm, uw_hbm, dw_hbm,
    lo_ref, gt_ref, gg_hbm, gu_hbm, gd_hbm,
    gw, uw, dw, gath0, gath1,
    part0, part1, core_in0, core_in1, pack0, pack1, x_in0, x_in1, y_out0, y_out1, y_in0, y_in1,
    far_out0, far_out1, far_in0, far_in1, acts0, acts1, p4, n_in, zpack, z_in, gg, gu, gd,
    load_sem, store_sem,
    tz_send, tz_recv, ty_send, ty_recv,
    sc_send, sc_recv, sx_send, sx_recv, sy_send, sy_recv, sf_send, sf_recv,
    ay_send, ay_recv, ax_send, ax_recv, ac_send, ac_recv,
    on_send, on_recv, oz_send, oz_recv,
):
    row, col, depth = lax.axis_index("row"), lax.axis_index("col"), lax.axis_index("depth")
    y_lo, z = lax.div(row, 16), lax.rem(row, 16)
    x, core = lax.div(depth, 2), lax.rem(depth, 2)
    d, ff = gw.shape
    gath = (gath0, gath1)
    far_out, far_in = (far_out0, far_out1), (far_in0, far_in1)
    part, core_in, pack = (part0, part1), (core_in0, core_in1), (pack0, pack1)
    x_in, y_out, y_in, acts = (x_in0, x_in1), (y_out0, y_out1), (y_in0, y_in1), (acts0, acts1)

    def z_dev(other):
        return (y_lo * 16 + other, col, depth)

    def col_dev(other):
        return (row, other, depth)

    def x_dev(other):
        return (row, col, other * 2 + core)

    next_dev = ((1 - y_lo) * 16 + z, col, depth)
    core_dev = (row, col, x * 2 + 1 - core)

    def remote(src, dst, send, recv, device):
        return pltpu.make_async_remote_copy(
            src_ref=src, dst_ref=dst, send_sem=send, recv_sem=recv,
            device_id=device, device_id_type=MESH,
        )

    def arrived(ref, recv):
        remote(ref, ref, load_sem.at[0], recv, core_dev).wait_recv()

    def left(ref, send):
        remote(ref, ref, send, load_sem.at[0], core_dev).wait_send()

    def col_at(q):
        return lax.rem(col + q, 4)

    def x_at(step):
        return lax.rem(x + step, 4)

    own_loads = [
        pltpu.make_async_copy(tok_hbm, gath0.at[row], load_sem.at[0]),
        pltpu.make_async_copy(grad_hbm, gath1.at[row], load_sem.at[1]),
    ]
    loads = [
        pltpu.make_async_copy(gw_hbm, gw, load_sem.at[2]),
        pltpu.make_async_copy(uw_hbm, uw, load_sem.at[3]),
        pltpu.make_async_copy(dw_hbm, dw, load_sem.at[4]),
    ]
    for load in own_loads + loads:
        load.start()

    barrier = pltpu.get_barrier_semaphore()

    def greet(device):
        pl.semaphore_signal(barrier, inc=1, device_id=device, device_id_type=MESH)

    for off in Z_NEAR:
        greet(z_dev(lax.rem(z + off, 16)))
    for step in FAR:
        greet(col_dev(col_at(step)))
        greet(x_dev(x_at(step)))
    greet(next_dev)
    greet(core_dev)
    for load in own_loads:
        load.wait()
    pl.semaphore_wait(barrier, 16)

    def pass_on(p, src_z):
        slot = gath[p].at[y_lo * 16 + src_z]
        remote(slot, slot, ty_send.at[p], ty_recv.at[p], next_dev).start()

    def gather_start(p):
        slot = gath[p].at[row]
        for off in Z_NEAR:
            remote(
                slot, slot, tz_send.at[p], tz_recv.at[p * 16 + z], z_dev(lax.rem(z + off, 16))
            ).start()
        pass_on(p, z)

    def gather_pass(p, offs):
        for off in offs:
            src_z = lax.rem(z + off, 16)
            slot = gath[p].at[y_lo * 16 + src_z]
            arrived(slot, tz_recv.at[p * 16 + src_z])
            if off in (12, 13, 14, 15) or off in (1, 2, 3):
                onward = 4 if off > 8 else 12
                remote(
                    slot, slot, tz_send.at[p], tz_recv.at[p * 16 + src_z], z_dev(lax.rem(z + onward, 16))
                ).start()
            pass_on(p, src_z)

    def gather_all(p):
        arrived(gath[p].at[pl.ds((1 - y_lo) * 16, 16)], ty_recv.at[p])
        return gath[p][...].astype(F32).reshape(256, d).astype(BF16)

    def col_of(p, j):
        if p:
            return col_at((FAR + (0,))[j])
        half = lax.rem(y_lo + j // 2, 2)
        apart = half - lax.div(col, 2)
        odd = lax.rem(col, 2)
        first = odd + (1 - apart * apart) * (1 - 2 * odd)
        return 2 * half + (first if j % 2 == 0 else 1 - first)

    def sums_start(p, j):
        chips = pl.ds(col_of(p, j) * 4, 4)
        remote(
            part[p].at[chips, 1 - core], core_in[p].at[chips],
            sc_send.at[p], sc_recv.at[p * 4 + j], core_dev,
        ).start()

    def sums_x(p, j):
        first = col_of(p, j) * 4
        chips = pl.ds(first, 4)
        arrived(core_in[p].at[chips], sc_recv.at[p * 4 + j])
        pack[p][chips] = (part[p][chips, core] + core_in[p][chips]).astype(BF16)
        for step in FAR:
            remote(
                pack[p].at[first + x_at(step)], x_in[p].at[first + x],
                sx_send.at[p], sx_recv.at[p * 4 + j], x_dev(x_at(step)),
            ).start()

    def sums_y(p, j):
        to = col_of(p, j)
        first = to * 4
        arrived(x_in[p].at[pl.ds(0, 3)], sx_recv.at[p * 4 + j])
        total = part[p][first + x, core] + core_in[p][first + x]
        for step in FAR:
            total = total + x_in[p][first + x_at(step)].astype(F32)
        y_out[p][to] = total
        away = lax.rem(to + 4 - col, 4)

        @pl.when(away == 2)
        def _():
            far_out[p][...] = total.astype(BF16)
            remote(far_out[p], far_in[p], sf_send.at[p], sf_recv.at[p], col_dev(to)).start()

        @pl.when(lax.rem(away, 2) == 1)
        def _():
            remote(y_out[p].at[to], y_in[p].at[col], sy_send.at[p], sy_recv.at[p], col_dev(to)).start()

    def sums_total(p):
        arrived(y_in[p].at[pl.ds(0, 2)], sy_recv.at[p])
        total = y_out[p][col] + y_in[p][col_at(1)] + y_in[p][col_at(3)]
        arrived(far_in[p], sf_recv.at[p])
        return total + far_in[p][...].astype(F32)

    def acts_x(p, q):
        slot = acts[p].at[col_at(q) * 4 + x, core]
        for step in FAR:
            remote(
                slot, slot, ax_send.at[p], ax_recv.at[p * 4 + col_at(q)], x_dev(x_at(step))
            ).start()

    def acts_start(p):
        slot = acts[p].at[col * 4 + x, core]
        for q in FAR:
            remote(slot, slot, ay_send.at[p], ay_recv.at[p * 4 + col], col_dev(col_at(q))).start()
        acts_x(p, 0)

    def acts_y(p, q):
        arrived(acts[p].at[col_at(q) * 4 + x, core], ay_recv.at[p * 4 + col_at(q)])
        acts_x(p, q)

    def acts_core(p, q):
        arrived(acts[p].at[pl.ds(0, 3), core], ax_recv.at[p * 4 + col_at(q)])
        group = acts[p].at[pl.ds(col_at(q) * 4, 4), core]
        remote(group, group, ac_send.at[p], ac_recv.at[p], core_dev).start()

    def acts_all(p):
        arrived(acts[p].at[:, core], ac_recv.at[p])

    z_hi, z_sub = lax.div(z, 4), lax.rem(z, 4)

    def out_start(p):
        for q in FAR + (0,):
            zs = pl.ds(lax.rem(z_hi + q, 4) * 4, 4)
            remote(
                p4.at[p, 1 - y_lo, zs], n_in.at[p, zs], on_send.at[p], on_recv.at[p * 4 + q], next_dev
            ).start()

    def out_z(p, q):
        first = lax.rem(z_hi + q, 4) * 4
        zs = pl.ds(first, 4)
        arrived(n_in.at[p, zs], on_recv.at[p * 4 + q])
        zpack[p, zs] = (p4[p, y_lo, zs] + n_in[p, zs]).astype(BF16)
        for step in FAR + (0,):
            if q or step:
                other = first + lax.rem(z_sub + step, 4)
                remote(
                    zpack.at[p, other], z_in.at[p, z], oz_send.at[p], oz_recv.at[p], z_dev(other)
                ).start()

    def out_all(p):
        arrived(z_in.at[p, pl.ds(0, 15)], oz_recv.at[p])
        total = p4[p, y_lo, z] + n_in[p, z]

        def body(i, total):
            return total + z_in[p, lax.rem(z + i, 16)].astype(F32)

        return lax.fori_loop(1, 16, body, total).astype(BF16)

    gather_start(0)
    gather_start(1)
    gather_pass(0, Z_NEAR[::-1])
    gather_pass(1, Z_NEAR[::-1])
    gather_pass(0, Z_FAR)
    for load in loads:
        load.wait()

    def gate_up(half):
        tok = gath0[pl.ds(half * 16, 16)].astype(F32).reshape(128, d).astype(BF16)
        chips = pl.ds(half * 8, 8)
        part0[chips, :, :, 0:ff] = dot(tok, gw[...], 1, 0).reshape(8, 2, 8, ff)
        part0[chips, :, :, ff:] = dot(tok, uw[...], 1, 0).reshape(8, 2, 8, ff)

    gate_up(y_lo)
    sums_start(0, 0)
    sums_start(0, 1)
    gather_pass(1, Z_FAR)
    sums_x(0, 0)
    sums_x(0, 1)
    arrived(gath0.at[pl.ds((1 - y_lo) * 16, 16)], ty_recv.at[0])
    gate_up(1 - y_lo)
    sums_start(0, 2)
    sums_start(0, 3)
    sums_x(0, 2)
    sums_x(0, 3)
    grad_all = gather_all(1)
    part1[...] = dot(grad_all, dw[...], 1, 1).reshape(16, 2, 8, ff)
    for j in range(4):
        sums_start(1, j)
    for j in range(4):
        sums_y(0, j)
    for j in range(4):
        sums_x(1, j)
    total = sums_total(0)
    gate_pre = total[:, 0:ff]
    up_proj = total[:, ff:]
    sig = jax.nn.sigmoid(gate_pre)
    acts0[col * 4 + x, core] = (gate_pre * sig * up_proj).astype(BF16)
    acts_start(0)
    for j in range(4):
        sums_y(1, j)
    for q in NEAR:
        acts_y(0, q)
    d_hidden = sums_total(1)
    acts1[col * 4 + x, core, :, 0:ff] = (
        d_hidden * up_proj * sig * (1.0 + gate_pre * (1.0 - sig))
    ).astype(BF16)
    acts1[col * 4 + x, core, :, ff:] = (d_hidden * gate_pre * sig).astype(BF16)
    acts_start(1)
    for q in (0,) + NEAR:
        acts_core(0, q)
    for q in NEAR:
        acts_y(1, q)
    acts_all(0)
    def out_terms(p, half):
        rows = acts[p][pl.ds(half * 8, 8)].astype(F32)
        if p == 0:
            term = dot(rows.reshape(128, ff).astype(BF16), dw[...], 1, 0)
        else:
            term = dot(rows[:, :, :, 0:ff].reshape(128, ff).astype(BF16), gw[...], 1, 1) + dot(
                rows[:, :, :, ff:].reshape(128, ff).astype(BF16), uw[...], 1, 1
            )
        p4[p, half] = term.reshape(16, 8, d)

    out_terms(0, 1 - y_lo)
    out_start(0)
    for q in (0, 1, 3):
        acts_core(1, q)
    out_terms(0, y_lo)
    acts_core(1, 2)
    for q in FAR + (0,):
        out_z(0, q)
    acts_all(1)
    out_terms(1, 1 - y_lo)
    out_start(1)
    out_terms(1, y_lo)
    d_gate = acts1[:, :, :, 0:ff].astype(F32).reshape(256, ff).astype(BF16)
    d_up = acts1[:, :, :, ff:].astype(F32).reshape(256, ff).astype(BF16)
    for q in FAR + (0,):
        out_z(1, q)
    hid = acts0[...].astype(F32).reshape(256, ff).astype(BF16)
    tok_all = gath0[...].astype(F32).reshape(256, d).astype(BF16)
    gg[...] = dot(tok_all, d_gate, 0, 0).astype(BF16)
    stores = [pltpu.make_async_copy(gg, gg_hbm, store_sem.at[0])]
    stores[0].start()
    gu[...] = dot(tok_all, d_up, 0, 0).astype(BF16)
    stores.append(pltpu.make_async_copy(gu, gu_hbm, store_sem.at[1]))
    stores[1].start()
    gd[...] = dot(hid, grad_all, 0, 0).astype(BF16)
    stores.append(pltpu.make_async_copy(gd, gd_hbm, store_sem.at[2]))
    stores[2].start()
    for p in (0, 1):
        left(gath[p].at[pl.ds(0, 15)], tz_send.at[p])
        left(gath[p].at[pl.ds(0, 16)], ty_send.at[p])
        left(core_in[p], sc_send.at[p])
        left(pack[p].at[pl.ds(0, 12)], sx_send.at[p])
        left(y_in[p].at[pl.ds(0, 2)], sy_send.at[p])
        left(far_in[p], sf_send.at[p])
        left(acts[p].at[pl.ds(0, 3), core], ay_send.at[p])
        left(acts[p].at[pl.ds(0, 12), core], ax_send.at[p])
        left(acts[p].at[:, core], ac_send.at[p])
        left(n_in.at[p], on_send.at[p])
    lo_ref[...] = out_all(0)
    gt_ref[...] = out_all(1)
    for p in (0, 1):
        left(zpack.at[p, pl.ds(0, 15)], oz_send.at[p])
    for store in stores:
        store.wait()


def land(*refs):
    sources, targets, held = refs[:5], refs[5:10], refs[10:15]
    in_sem, out_sem = refs[15:]
    loads = [
        pltpu.make_async_copy(source, buf, in_sem.at[i])
        for i, (source, buf) in enumerate(zip(sources, held))
    ]
    stores = [
        pltpu.make_async_copy(buf, target, out_sem.at[i])
        for i, (buf, target) in enumerate(zip(held, targets))
    ]
    for load in loads:
        load.start()
    for load, store in zip(loads, stores):
        load.wait()
        store.start()
    for store in stores:
        store.wait()


def per_device(tokens, grad_out, gate_weight, up_weight, down_weight):
    d, ff = gate_weight.shape
    vmem = pl.BlockSpec(memory_space=pltpu.VMEM)
    hbm = pl.BlockSpec(memory_space=pltpu.HBM)
    dma = pltpu.SemaphoreType.DMA
    results = pl.pallas_call(
        kernel,
        out_shape=(
            jax.ShapeDtypeStruct((8, d), BF16),
            jax.ShapeDtypeStruct((8, d), BF16),
            jax.ShapeDtypeStruct((d, ff), BF16),
            jax.ShapeDtypeStruct((d, ff), BF16),
            jax.ShapeDtypeStruct((ff, d), BF16),
        ),
        in_specs=[hbm] * 5,
        out_specs=(vmem, vmem, hbm, hbm, hbm),
        scratch_shapes=[
            pltpu.VMEM((d, ff), BF16),
            pltpu.VMEM((d, ff), BF16),
            pltpu.VMEM((ff, d), BF16),
            pltpu.VMEM((32, 8, d), BF16),
            pltpu.VMEM((32, 8, d), BF16),
            pltpu.VMEM((16, 2, 8, 2 * ff), F32),
            pltpu.VMEM((16, 2, 8, ff), F32),
            pltpu.VMEM((16, 8, 2 * ff), F32),
            pltpu.VMEM((16, 8, ff), F32),
            pltpu.VMEM((16, 8, 2 * ff), BF16),
            pltpu.VMEM((16, 8, ff), BF16),
            pltpu.VMEM((16, 8, 2 * ff), BF16),
            pltpu.VMEM((16, 8, ff), BF16),
            pltpu.VMEM((4, 8, 2 * ff), F32),
            pltpu.VMEM((4, 8, ff), F32),
            pltpu.VMEM((4, 8, 2 * ff), F32),
            pltpu.VMEM((4, 8, ff), F32),
            pltpu.VMEM((8, 2 * ff), BF16),
            pltpu.VMEM((8, ff), BF16),
            pltpu.VMEM((8, 2 * ff), BF16),
            pltpu.VMEM((8, ff), BF16),
            pltpu.VMEM((16, 2, 8, ff), BF16),
            pltpu.VMEM((16, 2, 8, 2 * ff), BF16),
            pltpu.VMEM((2, 2, 16, 8, d), F32),
            pltpu.VMEM((2, 16, 8, d), F32),
            pltpu.VMEM((2, 16, 8, d), BF16),
            pltpu.VMEM((2, 16, 8, d), BF16),
            pltpu.VMEM((d, ff), BF16),
            pltpu.VMEM((d, ff), BF16),
            pltpu.VMEM((ff, d), BF16),
            dma((5,)), dma((3,)),
            dma((2,)), dma((32,)), dma((2,)), dma((2,)),
            dma((2,)), dma((8,)), dma((2,)), dma((8,)), dma((2,)), dma((2,)), dma((2,)), dma((2,)),
            dma((2,)), dma((8,)), dma((2,)), dma((8,)), dma((2,)), dma((2,)),
            dma((2,)), dma((8,)), dma((2,)), dma((2,)),
        ],
        compiler_params=pltpu.CompilerParams(
            collective_id=0, has_side_effects=True, vmem_limit_bytes=62 << 20
        ),
        name="swiglu_exchange",
    )(tokens, grad_out, gate_weight, up_weight, down_weight)
    return pl.pallas_call(
        land,
        out_shape=tuple(jax.ShapeDtypeStruct(r.shape, r.dtype) for r in results),
        in_specs=[pl.BlockSpec(memory_space=pl.ANY)] * 5,
        out_specs=(pl.BlockSpec(memory_space=pl.ANY),) * 5,
        scratch_shapes=[pltpu.VMEM(r.shape, r.dtype) for r in results] + [dma((5,)), dma((5,))],
        name="land",
    )(*results)


def solution(mesh):
    acts = P("row", ("col", "depth"))
    weights = P(("col", "depth"), "row")
    return jax.shard_map(
        per_device,
        mesh=mesh,
        in_specs=(acts, acts, weights, weights, acts),
        out_specs=(acts, acts, weights, weights, acts),
        check_vma=False,
    )
```

```python
import functools
import jax
import jax.numpy as jnp
from jax import lax
from jax.experimental import pallas as pl
from jax.experimental.pallas import tpu as pltpu
from jax.sharding import PartitionSpec as P

MESH = pl.DeviceIdType.MESH
F32 = jnp.float32
BF16 = jnp.bfloat16
FAR = (2, 1, 3)
NEAR = (1, 3, 2)
Z_NEAR = (12, 4, 13, 3, 14, 2, 15, 1)
Z_FAR = (11, 5, 10, 6, 9, 7, 8)


def dot(left, right, left_dim, right_dim):
    return lax.dot_general(
        left, right, (((left_dim,), (right_dim,)), ((), ())), preferred_element_type=F32
    )


def kernel(
    tok_hbm, grad_hbm, gw_hbm, uw_hbm, dw_hbm,
    lo_ref, gt_ref, gg_hbm, gu_hbm, gd_hbm,
    gw, uw, dw, gath0, gath1,
    part0, part1, core_in0, core_in1, pack0, pack1, x_in0, x_in1, y_out0, y_out1, y_in0, y_in1,
    far_out0, far_out1, far_in0, far_in1, acts0, acts1, p4, n_in, zpack, z_in, gg, gu, gd,
    load_sem, store_sem,
    tz_send, tz_recv, ty_send, ty_recv,
    sc_send, sc_recv, sx_send, sx_recv, sy_send, sy_recv, sf_send, sf_recv,
    ay_send, ay_recv, ax_send, ax_recv, ac_send, ac_recv,
    on_send, on_recv, oz_send, oz_recv,
):
    row, col, depth = lax.axis_index("row"), lax.axis_index("col"), lax.axis_index("depth")
    y_lo, z = lax.div(row, 16), lax.rem(row, 16)
    x, core = lax.div(depth, 2), lax.rem(depth, 2)
    d, ff = gw.shape
    gath = (gath0, gath1)
    far_out, far_in = (far_out0, far_out1), (far_in0, far_in1)
    part, core_in, pack = (part0, part1), (core_in0, core_in1), (pack0, pack1)
    x_in, y_out, y_in, acts = (x_in0, x_in1), (y_out0, y_out1), (y_in0, y_in1), (acts0, acts1)

    def z_dev(other):
        return (y_lo * 16 + other, col, depth)

    def col_dev(other):
        return (row, other, depth)

    def x_dev(other):
        return (row, col, other * 2 + core)

    next_dev = ((1 - y_lo) * 16 + z, col, depth)
    core_dev = (row, col, x * 2 + 1 - core)

    def remote(src, dst, send, recv, device):
        return pltpu.make_async_remote_copy(
            src_ref=src, dst_ref=dst, send_sem=send, recv_sem=recv,
            device_id=device, device_id_type=MESH,
        )

    def arrived(ref, recv):
        remote(ref, ref, load_sem.at[0], recv, core_dev).wait_recv()

    def left(ref, send):
        remote(ref, ref, send, load_sem.at[0], core_dev).wait_send()

    def col_at(q):
        return lax.rem(col + q, 4)

    def x_at(step):
        return lax.rem(x + step, 4)

    own_loads = [
        pltpu.make_async_copy(tok_hbm, gath0.at[row], load_sem.at[0]),
        pltpu.make_async_copy(grad_hbm, gath1.at[row], load_sem.at[1]),
    ]
    loads = [
        pltpu.make_async_copy(gw_hbm, gw, load_sem.at[2]),
        pltpu.make_async_copy(uw_hbm, uw, load_sem.at[3]),
        pltpu.make_async_copy(dw_hbm, dw, load_sem.at[4]),
    ]
    for load in own_loads + loads:
        load.start()

    barrier = pltpu.get_barrier_semaphore()

    def greet(device):
        pl.semaphore_signal(barrier, inc=1, device_id=device, device_id_type=MESH)

    for off in Z_NEAR:
        greet(z_dev(lax.rem(z + off, 16)))
    for step in FAR:
        greet(col_dev(col_at(step)))
        greet(x_dev(x_at(step)))
    greet(next_dev)
    greet(core_dev)
    for load in own_loads:
        load.wait()
    pl.semaphore_wait(barrier, 16)

    def pass_on(p, src_z):
        slot = gath[p].at[y_lo * 16 + src_z]
        remote(slot, slot, ty_send.at[p], ty_recv.at[p], next_dev).start()

    def gather_start(p):
        slot = gath[p].at[row]
        for off in Z_NEAR:
            remote(
                slot, slot, tz_send.at[p], tz_recv.at[p * 16 + z], z_dev(lax.rem(z + off, 16))
            ).start()
        pass_on(p, z)

    def gather_pass(p, offs):
        for off in offs:
            src_z = lax.rem(z + off, 16)
            slot = gath[p].at[y_lo * 16 + src_z]
            arrived(slot, tz_recv.at[p * 16 + src_z])
            if off in (12, 13, 14, 15) or off in (1, 2, 3):
                onward = 4 if off > 8 else 12
                remote(
                    slot, slot, tz_send.at[p], tz_recv.at[p * 16 + src_z], z_dev(lax.rem(z + onward, 16))
                ).start()
            pass_on(p, src_z)

    def gather_all(p):
        arrived(gath[p].at[pl.ds((1 - y_lo) * 16, 16)], ty_recv.at[p])
        return gath[p][...].astype(F32).reshape(256, d).astype(BF16)

    def col_of(p, j):
        if p:
            return col_at((FAR + (0,))[j])
        half = lax.rem(y_lo + j // 2, 2)
        apart = half - lax.div(col, 2)
        odd = lax.rem(col, 2)
        first = odd + (1 - apart * apart) * (1 - 2 * odd)
        return 2 * half + (first if j % 2 == 0 else 1 - first)

    def sums_start(p, j):
        chips = pl.ds(col_of(p, j) * 4, 4)
        remote(
            part[p].at[chips, 1 - core], core_in[p].at[chips],
            sc_send.at[p], sc_recv.at[p * 4 + j], core_dev,
        ).start()

    def sums_x(p, j):
        first = col_of(p, j) * 4
        chips = pl.ds(first, 4)
        arrived(core_in[p].at[chips], sc_recv.at[p * 4 + j])
        pack[p][chips] = (part[p][chips, core] + core_in[p][chips]).astype(BF16)
        for step in FAR:
            remote(
                pack[p].at[first + x_at(step)], x_in[p].at[first + x],
                sx_send.at[p], sx_recv.at[p * 4 + j], x_dev(x_at(step)),
            ).start()

    def sums_y(p, j):
        to = col_of(p, j)
        first = to * 4
        arrived(x_in[p].at[pl.ds(0, 3)], sx_recv.at[p * 4 + j])
        total = part[p][first + x, core] + core_in[p][first + x]
        for step in FAR:
            total = total + x_in[p][first + x_at(step)].astype(F32)
        y_out[p][to] = total
        away = lax.rem(to + 4 - col, 4)

        @pl.when(away == 2)
        def _():
            far_out[p][...] = total.astype(BF16)
            remote(far_out[p], far_in[p], sf_send.at[p], sf_recv.at[p], col_dev(to)).start()

        @pl.when(lax.rem(away, 2) == 1)
        def _():
            remote(y_out[p].at[to], y_in[p].at[col], sy_send.at[p], sy_recv.at[p], col_dev(to)).start()

    def sums_total(p):
        arrived(y_in[p].at[pl.ds(0, 2)], sy_recv.at[p])
        total = y_out[p][col] + y_in[p][col_at(1)] + y_in[p][col_at(3)]
        arrived(far_in[p], sf_recv.at[p])
        return total + far_in[p][...].astype(F32)

    def acts_x(p, q):
        slot = acts[p].at[col_at(q) * 4 + x, core]
        for step in FAR:
            remote(
                slot, slot, ax_send.at[p], ax_recv.at[p * 4 + col_at(q)], x_dev(x_at(step))
            ).start()

    def acts_start(p):
        slot = acts[p].at[col * 4 + x, core]
        for q in FAR:
            remote(slot, slot, ay_send.at[p], ay_recv.at[p * 4 + col], col_dev(col_at(q))).start()
        acts_x(p, 0)

    def acts_y(p, q):
        arrived(acts[p].at[col_at(q) * 4 + x, core], ay_recv.at[p * 4 + col_at(q)])
        acts_x(p, q)

    def acts_core(p, q):
        arrived(acts[p].at[pl.ds(0, 3), core], ax_recv.at[p * 4 + col_at(q)])
        group = acts[p].at[pl.ds(col_at(q) * 4, 4), core]
        remote(group, group, ac_send.at[p], ac_recv.at[p], core_dev).start()

    def acts_all(p):
        arrived(acts[p].at[:, core], ac_recv.at[p])

    z_hi, z_sub = lax.div(z, 4), lax.rem(z, 4)

    def out_start(p):
        for q in FAR + (0,):
            zs = pl.ds(lax.rem(z_hi + q, 4) * 4, 4)
            remote(
                p4.at[p, 1 - y_lo, zs], n_in.at[p, zs], on_send.at[p], on_recv.at[p * 4 + q], next_dev
            ).start()

    def out_z(p, q):
        first = lax.rem(z_hi + q, 4) * 4
        zs = pl.ds(first, 4)
        arrived(n_in.at[p, zs], on_recv.at[p * 4 + q])
        zpack[p, zs] = (p4[p, y_lo, zs] + n_in[p, zs]).astype(BF16)
        for step in FAR + (0,):
            if q or step:
                other = first + lax.rem(z_sub + step, 4)
                remote(
                    zpack.at[p, other], z_in.at[p, z], oz_send.at[p], oz_recv.at[p], z_dev(other)
                ).start()

    def out_all(p):
        arrived(z_in.at[p, pl.ds(0, 15)], oz_recv.at[p])
        total = p4[p, y_lo, z] + n_in[p, z]

        def body(i, total):
            return total + z_in[p, lax.rem(z + i, 16)].astype(F32)

        return lax.fori_loop(1, 16, body, total).astype(BF16)

    gather_start(0)
    gather_start(1)
    gather_pass(0, Z_NEAR[::-1])
    gather_pass(1, Z_NEAR[::-1])
    gather_pass(0, Z_FAR)
    gather_pass(1, Z_FAR)
    for load in loads:
        load.wait()

    def gate_up(half):
        tok = gath0[pl.ds(half * 16, 16)].astype(F32).reshape(128, d).astype(BF16)
        chips = pl.ds(half * 8, 8)
        part0[chips, :, :, 0:ff] = dot(tok, gw[...], 1, 0).reshape(8, 2, 8, ff)
        part0[chips, :, :, ff:] = dot(tok, uw[...], 1, 0).reshape(8, 2, 8, ff)

    gate_up(y_lo)
    sums_start(0, 0)
    sums_start(0, 1)
    sums_x(0, 0)
    sums_x(0, 1)
    arrived(gath0.at[pl.ds((1 - y_lo) * 16, 16)], ty_recv.at[0])
    gate_up(1 - y_lo)
    sums_start(0, 2)
    sums_start(0, 3)
    sums_x(0, 2)
    sums_x(0, 3)
    grad_all = gather_all(1)
    part1[...] = dot(grad_all, dw[...], 1, 1).reshape(16, 2, 8, ff)
    for j in range(4):
        sums_start(1, j)
    for j in range(4):
        sums_y(0, j)
    for j in range(4):
        sums_x(1, j)
    total = sums_total(0)
    gate_pre = total[:, 0:ff]
    up_proj = total[:, ff:]
    sig = jax.nn.sigmoid(gate_pre)
    acts0[col * 4 + x, core] = (gate_pre * sig * up_proj).astype(BF16)
    acts_start(0)
    for j in range(4):
        sums_y(1, j)
    for q in NEAR:
        acts_y(0, q)
    d_hidden = sums_total(1)
    acts1[col * 4 + x, core, :, 0:ff] = (
        d_hidden * up_proj * sig * (1.0 + gate_pre * (1.0 - sig))
    ).astype(BF16)
    acts1[col * 4 + x, core, :, ff:] = (d_hidden * gate_pre * sig).astype(BF16)
    acts_start(1)
    for q in (0,) + NEAR:
        acts_core(0, q)
    for q in NEAR:
        acts_y(1, q)
    acts_all(0)
    def out_terms(p, half):
        rows = acts[p][pl.ds(half * 8, 8)].astype(F32)
        if p == 0:
            term = dot(rows.reshape(128, ff).astype(BF16), dw[...], 1, 0)
        else:
            term = dot(rows[:, :, :, 0:ff].reshape(128, ff).astype(BF16), gw[...], 1, 1) + dot(
                rows[:, :, :, ff:].reshape(128, ff).astype(BF16), uw[...], 1, 1
            )
        p4[p, half] = term.reshape(16, 8, d)

    out_terms(0, 1 - y_lo)
    out_start(0)
    for q in (0, 1, 3):
        acts_core(1, q)
    out_terms(0, y_lo)
    acts_core(1, 2)
    for q in FAR + (0,):
        out_z(0, q)
    acts_all(1)
    out_terms(1, 1 - y_lo)
    out_start(1)
    out_terms(1, y_lo)
    d_gate = acts1[:, :, :, 0:ff].astype(F32).reshape(256, ff).astype(BF16)
    d_up = acts1[:, :, :, ff:].astype(F32).reshape(256, ff).astype(BF16)
    for q in FAR + (0,):
        out_z(1, q)
    hid = acts0[...].astype(F32).reshape(256, ff).astype(BF16)
    tok_all = gath0[...].astype(F32).reshape(256, d).astype(BF16)
    gg[...] = dot(tok_all, d_gate, 0, 0).astype(BF16)
    stores = [pltpu.make_async_copy(gg, gg_hbm, store_sem.at[0])]
    stores[0].start()
    gu[...] = dot(tok_all, d_up, 0, 0).astype(BF16)
    stores.append(pltpu.make_async_copy(gu, gu_hbm, store_sem.at[1]))
    stores[1].start()
    gd[...] = dot(hid, grad_all, 0, 0).astype(BF16)
    stores.append(pltpu.make_async_copy(gd, gd_hbm, store_sem.at[2]))
    stores[2].start()
    for p in (0, 1):
        left(gath[p].at[pl.ds(0, 15)], tz_send.at[p])
        left(gath[p].at[pl.ds(0, 16)], ty_send.at[p])
        left(core_in[p], sc_send.at[p])
        left(pack[p].at[pl.ds(0, 12)], sx_send.at[p])
        left(y_in[p].at[pl.ds(0, 2)], sy_send.at[p])
        left(far_in[p], sf_send.at[p])
        left(acts[p].at[pl.ds(0, 3), core], ay_send.at[p])
        left(acts[p].at[pl.ds(0, 12), core], ax_send.at[p])
        left(acts[p].at[:, core], ac_send.at[p])
        left(n_in.at[p], on_send.at[p])
    lo_ref[...] = out_all(0)
    gt_ref[...] = out_all(1)
    for p in (0, 1):
        left(zpack.at[p, pl.ds(0, 15)], oz_send.at[p])
    for store in stores:
        store.wait()


def land(*refs):
    sources, targets, held = refs[:5], refs[5:10], refs[10:15]
    in_sem, out_sem = refs[15:]
    loads = [
        pltpu.make_async_copy(source, buf, in_sem.at[i])
        for i, (source, buf) in enumerate(zip(sources, held))
    ]
    stores = [
        pltpu.make_async_copy(buf, target, out_sem.at[i])
        for i, (buf, target) in enumerate(zip(held, targets))
    ]
    for load in loads:
        load.start()
    for load, store in zip(loads, stores):
        load.wait()
        store.start()
    for store in stores:
        store.wait()


def per_device(tokens, grad_out, gate_weight, up_weight, down_weight):
    d, ff = gate_weight.shape
    vmem = pl.BlockSpec(memory_space=pltpu.VMEM)
    hbm = pl.BlockSpec(memory_space=pltpu.HBM)
    dma = pltpu.SemaphoreType.DMA
    results = pl.pallas_call(
        kernel,
        out_shape=(
            jax.ShapeDtypeStruct((8, d), BF16),
            jax.ShapeDtypeStruct((8, d), BF16),
            jax.ShapeDtypeStruct((d, ff), BF16),
            jax.ShapeDtypeStruct((d, ff), BF16),
            jax.ShapeDtypeStruct((ff, d), BF16),
        ),
        in_specs=[hbm] * 5,
        out_specs=(vmem, vmem, hbm, hbm, hbm),
        scratch_shapes=[
            pltpu.VMEM((d, ff), BF16),
            pltpu.VMEM((d, ff), BF16),
            pltpu.VMEM((ff, d), BF16),
            pltpu.VMEM((32, 8, d), BF16),
            pltpu.VMEM((32, 8, d), BF16),
            pltpu.VMEM((16, 2, 8, 2 * ff), F32),
            pltpu.VMEM((16, 2, 8, ff), F32),
            pltpu.VMEM((16, 8, 2 * ff), F32),
            pltpu.VMEM((16, 8, ff), F32),
            pltpu.VMEM((16, 8, 2 * ff), BF16),
            pltpu.VMEM((16, 8, ff), BF16),
            pltpu.VMEM((16, 8, 2 * ff), BF16),
            pltpu.VMEM((16, 8, ff), BF16),
            pltpu.VMEM((4, 8, 2 * ff), F32),
            pltpu.VMEM((4, 8, ff), F32),
            pltpu.VMEM((4, 8, 2 * ff), F32),
            pltpu.VMEM((4, 8, ff), F32),
            pltpu.VMEM((8, 2 * ff), BF16),
            pltpu.VMEM((8, ff), BF16),
            pltpu.VMEM((8, 2 * ff), BF16),
            pltpu.VMEM((8, ff), BF16),
            pltpu.VMEM((16, 2, 8, ff), BF16),
            pltpu.VMEM((16, 2, 8, 2 * ff), BF16),
            pltpu.VMEM((2, 2, 16, 8, d), F32),
            pltpu.VMEM((2, 16, 8, d), F32),
            pltpu.VMEM((2, 16, 8, d), BF16),
            pltpu.VMEM((2, 16, 8, d), BF16),
            pltpu.VMEM((d, ff), BF16),
            pltpu.VMEM((d, ff), BF16),
            pltpu.VMEM((ff, d), BF16),
            dma((5,)), dma((3,)),
            dma((2,)), dma((32,)), dma((2,)), dma((2,)),
            dma((2,)), dma((8,)), dma((2,)), dma((8,)), dma((2,)), dma((2,)), dma((2,)), dma((2,)),
            dma((2,)), dma((8,)), dma((2,)), dma((8,)), dma((2,)), dma((2,)),
            dma((2,)), dma((8,)), dma((2,)), dma((2,)),
        ],
        compiler_params=pltpu.CompilerParams(
            collective_id=0, has_side_effects=True, vmem_limit_bytes=62 << 20
        ),
        name="swiglu_exchange",
    )(tokens, grad_out, gate_weight, up_weight, down_weight)
    return pl.pallas_call(
        land,
        out_shape=tuple(jax.ShapeDtypeStruct(r.shape, r.dtype) for r in results),
        in_specs=[pl.BlockSpec(memory_space=pl.ANY)] * 5,
        out_specs=(pl.BlockSpec(memory_space=pl.ANY),) * 5,
        scratch_shapes=[pltpu.VMEM(r.shape, r.dtype) for r in results] + [dma((5,)), dma((5,))],
        name="land",
    )(*results)


def solution(mesh):
    acts = P("row", ("col", "depth"))
    weights = P(("col", "depth"), "row")
    return jax.shard_map(
        per_device,
        mesh=mesh,
        in_specs=(acts, acts, weights, weights, acts),
        out_specs=(acts, acts, weights, weights, acts),
        check_vma=False,
    )
```
